32 devices in a mesh: wide: 8 (over z, core), narrow: 4 (over y, x).
Axes of the slice: x: 2, y: 2, z: 4, core: 2. Of those that a mesh axis runs over, the one named last changes fastest.
Arguments:
- normals: bfloat16 [3, 256, 1024, 512], P(None, 'wide', 'narrow'), may hold values from -6 to 6
- counts: int32 [256, 1024, 512], P('wide', 'narrow'), may hold values from 0 to 63
Outputs:
- spectrum: bfloat16 [512, 256, 1024], P(('wide', 'narrow'))
The draws below stay inside these ranges and needn't reach their ends.
Inputs may be any that keep to these rules, and one draw needn't show every extreme that they name: counts are splat sample counts of a cell.
All inputs are finite; a program needn't handle non-finite values.
Results may differ from the reference program's by a relative error of at most 0.0068.
Values may be sent and summed in bfloat16 or wider, within the bound.
No kernel may reach another device: no remote copies, remote signals or barrier semaphores. Data moves between devices by JAX's collectives and lax.ppermute only.
A program may use at most 192 MiB of HBM per device.

```python
import jax
import jax.numpy as jnp
from jax import lax

CX = 32
NY = 1024
NZ = 512
NX = 256


def set_ends(drawn, key, smallest, top_value):
    spot = [jax.random.randint(jax.random.fold_in(key, axis), (), 0, length) for axis, length in enumerate(drawn.shape)]
    longest = drawn.shape.index(max(drawn.shape))
    beside = spot[:longest] + [(spot[longest] + 1) % drawn.shape[longest]] + spot[longest + 1:]
    return drawn.at[tuple(spot)].set(smallest).at[tuple(beside)].set(top_value)


def steps_of(rng, extent, cuts, low, largest):
    loudness, own = 1.0, jax.random.fold_in(rng, 6)
    for axis_at, blocks in cuts:
        draws = jnp.exp(jax.random.uniform(jax.random.fold_in(own, axis_at), (blocks,), jnp.float32, low / len(cuts), largest / len(cuts)))
        loudness = loudness * jnp.repeat(draws, extent[axis_at] // blocks).reshape([-1 if axis == axis_at else 1 for axis in range(len(extent))])
    return loudness


def bell_draw(own_key, extent, scale, most, split=(), held_as=jnp.bfloat16):
    array = scale * jax.random.normal(own_key, extent, jnp.float32)
    if split:
        array = array * steps_of(own_key, extent, split, -0.22, 0.18)
    return jnp.clip(array, -most, most).astype(held_as)


def setup_inputs(seed: int = 0) -> dict:
    arg_keys = jax.random.split(jax.random.key(seed), 3)
    return {
        "normals": bell_draw(arg_keys[0], (3, NX, NY, NZ), 1.0, 6.0, ((1, 8), (2, 4))),
        "counts": set_ends(jax.random.randint(arg_keys[1], (NX, NY, NZ), 0, 64), jax.random.fold_in(arg_keys[1], 1), 0, 63).astype(jnp.int32),
    }


def cosine_table(size):
    freq = jnp.arange(size, dtype=jnp.float32)[:, None]
    place = jnp.arange(size, dtype=jnp.float32)[None, :]
    waves = jnp.cos(jnp.pi * (2.0 * place + 1.0) * freq / (2.0 * size))
    scales = jnp.where(freq == 0.0, jnp.sqrt(1.0 / size), jnp.sqrt(2.0 / size))
    return (scales * waves).astype(jnp.bfloat16)

def weight_of(count_block):
    values = count_block.astype(jnp.float32)
    return values / (values + 4.0)

def edge_flux(normals, counts, index):
    valid = jnp.logical_and(index >= 0, index < NX)
    clipped = jnp.clip(index, 0, NX - 1).astype(jnp.int32)
    count_row = lax.dynamic_slice_in_dim(counts, clipped, 1, 0)
    normal_row = lax.dynamic_slice_in_dim(normals[0], clipped, 1, 0)
    flux = weight_of(count_row) * normal_row.astype(jnp.float32)
    return jnp.where(valid, flux, jnp.zeros_like(flux))

def reference(normals, counts):
    table_z = cosine_table(NZ).astype(jnp.float32)
    table_y = cosine_table(NY).astype(jnp.float32)

    def one_block(block):
        start = (block * CX).astype(jnp.int32)
        weight = weight_of(lax.dynamic_slice_in_dim(counts, start, CX, 0))
        local = lax.dynamic_slice_in_dim(normals, start, CX, 1).astype(jnp.float32)
        flux_x = weight * local[0]
        before = edge_flux(normals, counts, start - 1)
        after = edge_flux(normals, counts, start + CX)
        extended = jnp.concatenate([before, flux_x, after], axis=0)
        diff_x = extended[2:] - extended[:-2]
        flux_y = weight * local[1]
        padded_y = jnp.pad(flux_y, ((0, 0), (1, 1), (0, 0)))
        diff_y = padded_y[:, 2:] - padded_y[:, :-2]
        flux_z = weight * local[2]
        padded_z = jnp.pad(flux_z, ((0, 0), (0, 0), (1, 1)))
        diff_z = padded_z[:, :, 2:] - padded_z[:, :, :-2]
        divergence = (0.5 * (diff_x + diff_y + diff_z)).astype(jnp.bfloat16)
        along_z = jnp.einsum('kn,xyn->kxy', table_z, divergence.astype(jnp.float32)).astype(jnp.bfloat16)
        return jnp.einsum('kxj,qj->kxq', along_z.astype(jnp.float32), table_y).astype(jnp.bfloat16)
    pieces = lax.map(one_block, jnp.arange(NX // CX, dtype=jnp.int32))
    return jnp.transpose(pieces, (1, 0, 2, 3)).reshape(NZ, NX, NY)
```

```python
import functools

import jax
import jax.numpy as jnp
import ml_dtypes
import numpy as np
from jax import lax
from jax.experimental import pallas as pl
from jax.experimental.pallas import tpu as pltpu
from jax.sharding import PartitionSpec as P

VMEM_BYTES = 56 * 1024 * 1024
PAD = 8


def cosine_table(size):
    freq = np.arange(size, dtype=np.float64)[:, None]
    place = np.arange(size, dtype=np.float64)[None, :]
    waves = np.cos(np.pi * (2.0 * place + 1.0) * freq / (2.0 * size))
    scales = np.where(freq == 0.0, np.sqrt(1.0 / size), np.sqrt(2.0 / size))
    return (scales * waves).astype(ml_dtypes.bfloat16)


def weight_of(counts):
    values = counts.astype(jnp.float32)
    return values / (values + 4.0)


def strip_rows(rows):
    return 32 if rows % 32 == 0 else 8


def planes_kernel(start, planes, total, normals, counts, low_y, high_y, low_x, high_x, table, out,
                  flux_y, weights, last_x, partial, divergence):
    step = pl.program_id(0)
    plane = jnp.clip(start - 1 + step, 0, total - 1)
    rows, depth = weights.shape
    strip = strip_rows(rows)
    strips = [slice(r, r + strip) for r in range(0, rows, strip)]

    for at in strips:
        weight = weight_of(counts[0, at, :])
        weights[at, :] = weight
        flux_y[PAD + at.start:PAD + at.stop, :] = weight * normals[1, 0, at, :].astype(jnp.float32)
    flux_y[PAD - 1:PAD, :] = low_y[pl.ds(plane, 1), :]
    flux_y[PAD + rows:PAD + rows + 1, :] = high_y[pl.ds(plane, 1), :]

    lane = lax.broadcasted_iota(jnp.int32, (strip, depth), 1)
    for at in strips:
        weight = weights[at, :]
        flux_x = weight * normals[0, 0, at, :].astype(jnp.float32)
        if start == 0:
            flux_x = jnp.where(step == 0, low_x[at, :].astype(jnp.float32), flux_x)
        if start + planes == total:
            flux_x = jnp.where(step == planes + 1, high_x[at, :].astype(jnp.float32), flux_x)
        flux_z = weight * normals[2, 0, at, :].astype(jnp.float32)
        after_z = jnp.where(lane == depth - 1, 0.0, pltpu.roll(flux_z, depth - 1, 1))
        before_z = jnp.where(lane == 0, 0.0, pltpu.roll(flux_z, 1, 1))
        diff_y = flux_y[PAD + at.start + 1:PAD + at.stop + 1, :] - flux_y[PAD + at.start - 1:PAD + at.stop - 1, :]
        divergence[at, :] = (0.5 * (flux_x + partial[at, :])).astype(jnp.bfloat16)
        partial[at, :] = diff_y + (after_z - before_z) - last_x[at, :]
        last_x[at, :] = flux_x

    @pl.when(step >= 2)
    def _():
        along = lax.dot_general(
            table[...], divergence[...], (((1,), (1,)), ((), ())), preferred_element_type=jnp.float32
        ).astype(jnp.bfloat16)
        out[:, 0] = along.reshape(out.shape[0], out.shape[2], rows)


def along_z_of(normals, counts, halos, table, start, planes, groups):
    _, total, rows, depth = normals.shape

    def plane_at(step):
        return jnp.clip(start - 1 + step, 0, total - 1)

    whole = pl.BlockSpec((rows, depth), lambda step: (0, 0))
    lines = pl.BlockSpec((total, depth), lambda step: (0, 0))
    size = planes * rows * depth
    return pl.pallas_call(
        functools.partial(planes_kernel, start, planes, total),
        grid=(planes + 2,),
        in_specs=[
            pl.BlockSpec((3, 1, rows, depth), lambda step: (0, plane_at(step), 0, 0)),
            pl.BlockSpec((1, rows, depth), lambda step: (plane_at(step), 0, 0)),
            lines,
            lines,
            whole,
            whole,
            pl.BlockSpec((depth, depth), lambda step: (0, 0)),
        ],
        out_specs=pl.BlockSpec((groups, 1, depth // groups, rows), lambda step: (0, jnp.maximum(step - 2, 0), 0, 0)),
        out_shape=jax.ShapeDtypeStruct((groups, planes, depth // groups, rows), jnp.bfloat16),
        scratch_shapes=[
            pltpu.VMEM((rows + 2 * PAD, depth), jnp.float32),
            pltpu.VMEM((rows, depth), jnp.float32),
            pltpu.VMEM((rows, depth), jnp.float32),
            pltpu.VMEM((rows, depth), jnp.float32),
            pltpu.VMEM((rows, depth), jnp.bfloat16),
        ],
        compiler_params=pltpu.CompilerParams(vmem_limit_bytes=VMEM_BYTES),
        cost_estimate=pl.CostEstimate(flops=2 * size * depth, bytes_accessed=12 * size, transcendentals=size),
    )(normals, counts, *halos, table)


def y_kernel(arrived, table, order, *rest):
    out = rest[-1]
    tiles, planes, slab, rows = arrived.shape
    total = jnp.zeros((planes * slab, table.shape[1]), jnp.float32)
    for tile in range(tiles):
        total += jnp.dot(
            arrived[tile].reshape(planes * slab, rows),
            table[tile * rows:(tile + 1) * rows, :],
            preferred_element_type=jnp.float32,
        )
    moved = jnp.dot(order[...], total.astype(jnp.bfloat16), preferred_element_type=jnp.float32)
    out[...] = moved.astype(jnp.bfloat16).reshape(slab, planes, table.shape[1])


def along_y_of(arrived, table, so_far, start, total, wide, narrow):
    _, planes, slab, rows = arrived.shape
    full_y = table.shape[1]
    count = planes * slab
    order = np.zeros((slab, planes, planes, slab), np.float32)
    for k in range(slab):
        for i in range(planes):
            order[k, i, i, k] = 1.0
    order = jnp.asarray(order.reshape(count, count).astype(ml_dtypes.bfloat16))
    operands = [arrived, table, order]
    in_specs = [
        pl.BlockSpec((narrow, planes, slab, rows), lambda at: (at, 0, 0, 0)),
        pl.BlockSpec(table.shape, lambda at: (0, 0)),
        pl.BlockSpec(order.shape, lambda at: (0, 0)),
    ]
    aliases = {}
    if so_far is not None:
        operands.append(so_far)
        in_specs.append(pl.BlockSpec(memory_space=pl.ANY))
        aliases = {3: 0}
    size = wide * count * full_y
    return pl.pallas_call(
        y_kernel,
        grid=(wide,),
        in_specs=in_specs,
        out_specs=pl.BlockSpec((slab, planes, full_y), lambda at: (0, at * (total // planes) + start // planes, 0)),
        out_shape=jax.ShapeDtypeStruct((slab, wide * total, full_y), jnp.bfloat16),
        input_output_aliases=aliases,
        compiler_params=pltpu.CompilerParams(vmem_limit_bytes=VMEM_BYTES),
        cost_estimate=pl.CostEstimate(flops=2 * size * (full_y + count), bytes_accessed=4 * size, transcendentals=0),
    )(*operands)


def halos_of(normals, counts):
    wide = lax.axis_size("wide")
    narrow = lax.axis_size("narrow")
    up = lambda count: [(i, i + 1) for i in range(count - 1)]
    down = lambda count: [(i + 1, i) for i in range(count - 1)]
    edge_y = lambda at: weight_of(counts[:, at, :]) * normals[1, :, at, :].astype(jnp.float32)
    edge_x = lambda at: (weight_of(counts[at]) * normals[0, at].astype(jnp.float32)).astype(jnp.bfloat16)
    return (
        lax.ppermute(edge_y(counts.shape[1] - 1), "narrow", up(narrow)),
        lax.ppermute(edge_y(0), "narrow", down(narrow)),
        lax.ppermute(edge_x(counts.shape[0] - 1), "wide", up(wide)),
        lax.ppermute(edge_x(0), "wide", down(wide)),
    )


def per_device(normals, counts):
    wide = lax.axis_size("wide")
    narrow = lax.axis_size("narrow")
    _, total, rows, depth = normals.shape
    full_y = narrow * rows
    slab = depth // (wide * narrow)
    halos = halos_of(normals, counts)
    table_z = jnp.asarray(cosine_table(depth))
    table_y = jnp.asarray(np.ascontiguousarray(cosine_table(full_y).T))
    if slab % 16 == 0:
        planes = 8
        quarter = total // planes
        starts = [((at + 1) % quarter) * planes for at in range(quarter)]
        spectrum = None
        for start in starts:
            along = along_z_of(normals, counts, halos, table_z, start, planes, wide * narrow)
            arrived = lax.all_to_all(along, ("wide", "narrow"), split_axis=0, concat_axis=0, tiled=True)
            spectrum = along_y_of(arrived, table_y, spectrum, start, total, wide, narrow)
        return spectrum
    along = along_z_of(normals, counts, halos, table_z, 0, total, 1)
    along = along.reshape(total, wide * narrow, slab, rows)
    arrived = lax.all_to_all(along, ("wide", "narrow"), split_axis=1, concat_axis=1, tiled=True)
    arrived = arrived.reshape(total, wide, narrow, slab, rows)
    pencil = jnp.transpose(arrived, (3, 1, 0, 2, 4)).reshape(slab * wide * total, full_y)
    spectrum = jnp.dot(pencil, table_y, preferred_element_type=jnp.float32).astype(jnp.bfloat16)
    return spectrum.reshape(slab, wide * total, full_y)


def solution(mesh):
    placed = (P(None, "wide", "narrow", None), P("wide", "narrow", None))
    return jax.shard_map(
        per_device,
        mesh=mesh,
        in_specs=placed,
        out_specs=P(("wide", "narrow"), None, None),
        check_vma=False,
    )
```

```python
import functools

import jax
import jax.numpy as jnp
import ml_dtypes
import numpy as np
from jax import lax
from jax.experimental import pallas as pl
from jax.experimental.pallas import tpu as pltpu
from jax.sharding import PartitionSpec as P

VMEM_BYTES = 56 * 1024 * 1024
PAD = 8
LANES = 128


def cosine_table(size):
    freq = np.arange(size, dtype=np.float64)[:, None]
    place = np.arange(size, dtype=np.float64)[None, :]
    waves = np.cos(np.pi * (2.0 * place + 1.0) * freq / (2.0 * size))
    scales = np.where(freq == 0.0, np.sqrt(1.0 / size), np.sqrt(2.0 / size))
    return (scales * waves).astype(ml_dtypes.bfloat16)


def weight_of(counts):
    values = counts.astype(jnp.float32)
    return values / (values + 4.0)


def strip_rows(rows):
    return 32 if rows % 32 == 0 else 8


def partner(index, step):
    return index ^ step


def device():
    return lax.axis_index("wide") * lax.axis_size("narrow") + lax.axis_index("narrow")


def planes_kernel(start, planes, total, block, sizes, normals, counts, low_y, high_y, low, high, low_counts,
                  high_counts, table, *rest):
    *outs, flux_y, last_x, partial, divergence, ordered = rest
    step = pl.program_id(0)
    steps = planes // block
    rows, depth = last_x.shape
    strip = strip_rows(rows)
    strips = [slice(r, r + strip) for r in range(0, rows, strip)]
    columns = [slice(c, c + LANES) for c in range(0, depth, LANES)]
    now = lax.rem(step, 2)
    before = 1 - now

    @pl.when(step == 0)
    def _():
        if sizes is None:
            ordered[...] = table[...]
        else:
            far, near = sizes
            slab = depth // (far * near)
            for place in range(near):
                for turn in range(far):
                    owner = partner(device() // near, turn) * near + partner(device() % near, place)
                    into = (place * far + turn) * slab
                    ordered[into:into + slab, :] = table[pl.ds(pl.multiple_of(owner * slab, slab), slab), :]
        for at in strips:
            if start == 0:
                last_x[at, :] = low[at, :].astype(jnp.float32)
            else:
                last_x[at, :] = weight_of(low_counts[0, at, :]) * low[0, 0, at, :].astype(jnp.float32)

    def transform(plane):
        along = lax.dot_general(
            ordered[...], divergence[plane], (((1,), (1,)), ((), ())), preferred_element_type=jnp.float32
        ).astype(jnp.bfloat16)
        share = depth // len(outs)
        for at, out in enumerate(outs):
            out[:, plane] = along[at * share:(at + 1) * share].reshape(out.shape[0], out.shape[2], rows)

    def diff_y(slot, plane, tile, at):
        after_y = flux_y[slot, plane, tile, PAD + at.start + 1:PAD + at.stop + 1, :]
        return after_y - flux_y[slot, plane, tile, PAD + at.start - 1:PAD + at.stop - 1, :]

    lane = lax.broadcasted_iota(jnp.int32, (strip, LANES), 1)
    first, last = lane == 0, lane == LANES - 1

    def take_in(at):
        ahead = []
        for plane in range(block):
            flux_x, before_z, after_z = [], [], []
            for tile, cut in enumerate(columns):
                weight = weight_of(counts[plane, at, cut])
                flux_x.append(weight * normals[0, plane, at, cut].astype(jnp.float32))
                flux_y[now, plane, tile, PAD + at.start:PAD + at.stop, :] = (
                    weight * normals[1, plane, at, cut].astype(jnp.float32)
                )
                flux_z = weight * normals[2, plane, at, cut].astype(jnp.float32)
                before_z.append(pltpu.roll(flux_z, 1, 1))
                after_z.append(pltpu.roll(flux_z, LANES - 1, 1))
            for tile, cut in enumerate(columns):
                left = before_z[tile - 1] if tile > 0 else 0.0
                right = after_z[tile + 1] if tile + 1 < len(columns) else 0.0
                diff_z = jnp.where(last, right, after_z[tile]) - jnp.where(first, left, before_z[tile])
                if plane == 0:
                    partial[block, at, cut] = partial[block - 1, at, cut] + flux_x[tile]
                    partial[0, at, cut] = diff_z - last_x[at, cut]
                else:
                    partial[plane - 1, at, cut] = partial[plane - 1, at, cut] + flux_x[tile]
                    partial[plane, at, cut] = diff_z - ahead[tile]
                if plane == block - 1:
                    last_x[at, cut] = flux_x[tile]
            ahead = flux_x

    def put_out(at):
        for tile, cut in enumerate(columns):
            done = partial[block, at, cut] + diff_y(before, block - 1, tile, at)
            divergence[block - 1, at, cut] = done.astype(jnp.bfloat16)
            for plane in range(block - 1):
                done = partial[plane, at, cut] + diff_y(now, plane, tile, at)
                divergence[plane, at, cut] = done.astype(jnp.bfloat16)

    @pl.when(step < steps)
    def _():
        for plane in range(block - 1):
            transform(plane)
        for plane in range(block):
            low_line = low_y[pl.ds(start + step * block + plane, 1), :]
            high_line = high_y[pl.ds(start + step * block + plane, 1), :]
            for tile, cut in enumerate(columns):
                flux_y[now, plane, tile, PAD - 1:PAD, :] = low_line[:, cut]
                flux_y[now, plane, tile, PAD + rows:PAD + rows + 1, :] = high_line[:, cut]
        for number, at in enumerate(strips):
            take_in(at)
            if number:
                put_out(strips[number - 1])
        put_out(strips[-1])
        transform(block - 1)

    @pl.when(step == steps)
    def _():
        for plane in range(block - 1):
            transform(plane)
        for at in strips:
            for tile, cut in enumerate(columns):
                if start + planes == total:
                    flux_x = high[at, cut].astype(jnp.float32)
                else:
                    flux_x = weight_of(high_counts[0, at, cut]) * high[0, 0, at, cut].astype(jnp.float32)
                done = flux_x + (partial[block - 1, at, cut] + diff_y(before, block - 1, tile, at))
                divergence[block - 1, at, cut] = done.astype(jnp.bfloat16)
        transform(block - 1)


def along_z_of(normals, counts, halos, table, start, planes, count=1, groups=1, sizes=None):
    _, total, rows, depth = normals.shape
    low_y, high_y, low_x, high_x = halos
    block = 4 if planes % 4 == 0 else 1
    steps = planes // block

    def block_at(step):
        return start // block + jnp.minimum(step, steps - 1)

    def edge(plane):
        return pl.BlockSpec((1, 1, rows, depth), lambda step: (0, plane, 0, 0))

    def edge_counts(plane):
        return pl.BlockSpec((1, rows, depth), lambda step: (plane, 0, 0))

    whole = pl.BlockSpec((rows, depth), lambda step: (0, 0))
    lines = pl.BlockSpec((total, depth), lambda step: (0, 0))
    at_low, at_high = start == 0, start + planes == total
    below, above = max(start - 1, 0), min(start + planes, total - 1)
    size = planes * rows * depth
    share = depth // (groups * count)
    return pl.pallas_call(
        functools.partial(planes_kernel, start, planes, total, block, sizes),
        grid=(steps + 1,),
        in_specs=[
            pl.BlockSpec((3, block, rows, depth), lambda step: (0, block_at(step), 0, 0)),
            pl.BlockSpec((block, rows, depth), lambda step: (block_at(step), 0, 0)),
            lines,
            lines,
            whole if at_low else edge(below),
            whole if at_high else edge(above),
            edge_counts(below),
            edge_counts(above),
            pl.BlockSpec((depth, depth), lambda step: (0, 0)),
        ],
        out_specs=[
            pl.BlockSpec((groups, block, share, rows), lambda step: (0, jnp.maximum(step - 1, 0), 0, 0))
        ] * count,
        out_shape=[jax.ShapeDtypeStruct((groups, planes, share, rows), jnp.bfloat16)] * count,
        scratch_shapes=[
            pltpu.VMEM((2, block, depth // LANES, rows + 2 * PAD, LANES), jnp.float32),
            pltpu.VMEM((rows, depth), jnp.float32),
            pltpu.VMEM((block + 1, rows, depth), jnp.float32),
            pltpu.VMEM((block, rows, depth), jnp.bfloat16),
            pltpu.VMEM((depth, depth), jnp.bfloat16),
        ],
        compiler_params=pltpu.CompilerParams(vmem_limit_bytes=VMEM_BYTES),
        cost_estimate=pl.CostEstimate(flops=2 * size * depth, bytes_accessed=12 * size, transcendentals=size),
    )(normals, counts, low_y, high_y, low_x if at_low else normals, high_x if at_high else normals, counts, counts, table)


def order_of(planes, slab):
    order = np.zeros((slab, planes, planes, slab), np.float32)
    for k in range(slab):
        for i in range(planes):
            order[k, i, i, k] = 1.0
    return jnp.asarray(order.reshape(planes * slab, planes * slab).astype(ml_dtypes.bfloat16))


def y_of(groups, table, order):
    planes, slab, rows = groups[0][0].shape
    count = planes * slab
    lines = [
        jnp.concatenate([tile[...].reshape(count, rows) for tile in tiles], axis=1) for tiles in groups
    ]
    along = jnp.dot(jnp.concatenate(lines, axis=0), table[...], preferred_element_type=jnp.float32)
    along = along.astype(jnp.bfloat16)
    moved = []
    for at in range(len(groups)):
        part = jnp.dot(order[...], along[at * count:(at + 1) * count], preferred_element_type=jnp.float32)
        moved.append(part.astype(jnp.bfloat16).reshape(slab, planes, table.shape[1]))
    return moved


def near_kernel(near, narrow, *refs):
    tiles, (table, order), (*outs, ordered) = refs[:near], refs[near:near + 2], refs[near + 2:]
    planes, _, rows = tiles[0].shape

    @pl.when(pl.program_id(0) == 0)
    def _():
        for place in range(narrow):
            owner = partner(device() % narrow, place)
            ordered[place * rows:(place + 1) * rows, :] = table[pl.ds(pl.multiple_of(owner * rows, rows), rows), :]

    moved = y_of([tiles[at:at + narrow] for at in range(0, near, narrow)], ordered, order)
    for step, out in enumerate(outs):

        @pl.when(pl.program_id(0) == step)
        def _():
            for core, part in enumerate(moved):
                out[:, core * planes:(core + 1) * planes, :] = part


def far_kernel(narrow, tiles, table, order, out):
    groups = [[tiles.at[at + place] for place in range(narrow)] for at in range(0, tiles.shape[0], narrow)]
    for at, moved in enumerate(y_of(groups, table, order)):
        out[:, at, :moved.shape[1]] = moved


def y_cost(planes, slab, wide, full_y):
    size = planes * slab * wide * full_y
    return pl.CostEstimate(flops=2 * size * (full_y + planes * slab), bytes_accessed=4 * size, transcendentals=0)


def along_y_near(tiles, table, far, narrow):
    planes, share, rows = tiles[0].shape
    near = len(tiles)
    slab = share // far
    full_y = table.shape[1]
    count = planes * slab
    cores = near // narrow
    return pl.pallas_call(
        functools.partial(near_kernel, near, narrow),
        grid=(far,),
        in_specs=[pl.BlockSpec((planes, slab, rows), lambda step: (0, step, 0))] * near + [
            pl.BlockSpec(table.shape, lambda step: (0, 0)),
            pl.BlockSpec((count, count), lambda step: (0, 0)),
        ],
        out_specs=[pl.BlockSpec((slab, cores * planes, full_y), lambda step: (0, 0, 0))] * far,
        out_shape=[jax.ShapeDtypeStruct((slab, cores * planes, full_y), jnp.bfloat16)] * far,
        scratch_shapes=[pltpu.VMEM(table.shape, jnp.bfloat16)],
        compiler_params=pltpu.CompilerParams(vmem_limit_bytes=VMEM_BYTES),
        cost_estimate=y_cost(planes, slab, far * cores, full_y),
    )(*tiles, table, order_of(planes, slab))


def along_y_far(tiles, table, total, narrow):
    count, planes, slab, rows = tiles.shape
    wide = count // narrow
    full_y = table.shape[1]
    return pl.pallas_call(
        functools.partial(far_kernel, narrow),
        grid=(wide // 2,),
        in_specs=[
            pl.BlockSpec((2 * narrow, planes, slab, rows), lambda at: (at, 0, 0, 0)),
            pl.BlockSpec(table.shape, lambda at: (0, 0)),
            pl.BlockSpec((planes * slab, planes * slab), lambda at: (0, 0)),
        ],
        out_specs=pl.BlockSpec((slab, 2, total, full_y), lambda at: (0, at, 0, 0)),
        out_shape=jax.ShapeDtypeStruct((slab, wide, total, full_y), jnp.bfloat16),
        compiler_params=pltpu.CompilerParams(vmem_limit_bytes=VMEM_BYTES),
        cost_estimate=y_cost(planes, slab, wide, full_y),
    )(tiles, table, order_of(planes, slab)).reshape(slab, wide * total, full_y)


def after(array, *others):
    return lax.optimization_barrier((array, *others))[0]


def swap_far(array, step, near):
    if step == 0:
        return array
    count = lax.axis_size("wide") * lax.axis_size("narrow")
    pairs = [(i, partner(i // near, step) * near + i % near) for i in range(count)]
    return lax.ppermute(array, ("wide", "narrow"), pairs)


def swap_near(array, step, near):
    if step == 0:
        return array
    count = lax.axis_size("wide") * lax.axis_size("narrow")
    pairs = [(i, i // near * near + partner(i % near, step)) for i in range(count)]
    return lax.ppermute(array, ("wide", "narrow"), pairs)


def halos_of(normals, counts):
    wide = lax.axis_size("wide")
    narrow = lax.axis_size("narrow")
    up = lambda count: [(i, i + 1) for i in range(count - 1)]
    down = lambda count: [(i + 1, i) for i in range(count - 1)]
    edge_y = lambda at: weight_of(counts[:, at, :]) * normals[1, :, at, :].astype(jnp.float32)
    edge_x = lambda at: (weight_of(counts[at]) * normals[0, at].astype(jnp.float32)).astype(jnp.bfloat16)
    low_y = lax.ppermute(edge_y(counts.shape[1] - 1), "narrow", up(narrow))
    high_y = lax.ppermute(edge_y(0), "narrow", down(narrow))
    low_x = lax.ppermute(edge_x(counts.shape[0] - 1), "wide", up(wide))
    high_x = lax.ppermute(edge_x(0), "wide", down(wide))
    return low_y, high_y, low_x, high_x


def per_device(normals, counts):
    wide = lax.axis_size("wide")
    narrow = lax.axis_size("narrow")
    _, total, rows, depth = normals.shape
    full_y = narrow * rows
    slab = depth // (wide * narrow)
    halos = halos_of(normals, counts)
    table_z = jnp.asarray(cosine_table(depth) * ml_dtypes.bfloat16(0.5))
    table_y = jnp.asarray(np.ascontiguousarray(cosine_table(full_y).T))
    cores = 2
    far = wide // cores
    near = cores * narrow
    if slab % 16 == 0 and total % 32 == 0 and wide == cores * far and far & (far - 1) == 0 and near & (near - 1) == 0:
        most = total * 3 // 4
        rest = total - most
        pieces = along_z_of(normals, counts, halos, after(table_z, halos[3]), 0, most, 1, wide * narrow)[0]
        later = after(table_z, pieces)
        pieces = lax.all_to_all(pieces, ("wide", "narrow"), split_axis=0, concat_axis=0, tiled=True)
        tiles = along_z_of(normals, counts, halos, later, most, rest, near, 1, (far, near))
        tiles = [swap_near(tile[0], step, near) for step, tile in enumerate(tiles)]
        far_pieces = along_y_near(tiles, table_y, far, narrow)
        pieces = after(pieces, far_pieces[0])
        far_pieces = [swap_far(piece, step, near) for step, piece in enumerate(far_pieces)]
        spectrum = along_y_far(pieces, table_y, total, narrow)
        mine = device() // near
        for step, piece in enumerate(far_pieces):
            for turn in range(cores):
                core = partner(device() % near // narrow, turn)
                at = (partner(mine, step) * cores + core) * total + most
                spectrum = lax.dynamic_update_slice(spectrum, piece[:, turn * rest:(turn + 1) * rest], (0, at, 0))
        return spectrum
    along = along_z_of(normals, counts, halos, table_z, 0, total)[0]
    along = along.reshape(total, wide * narrow, slab, rows)
    arrived = lax.all_to_all(along, ("wide", "narrow"), split_axis=1, concat_axis=1, tiled=True)
    arrived = arrived.reshape(total, wide, narrow, slab, rows)
    pencil = jnp.transpose(arrived, (3, 1, 0, 2, 4)).reshape(slab * wide * total, full_y)
    spectrum = jnp.dot(pencil, table_y, preferred_element_type=jnp.float32).astype(jnp.bfloat16)
    return spectrum.reshape(slab, wide * total, full_y)


def solution(mesh):
    placed = (P(None, "wide", "narrow", None), P("wide", "narrow", None))
    return jax.shard_map(
        per_device,
        mesh=mesh,
        in_specs=placed,
        out_specs=P(("wide", "narrow"), None, None),
        check_vma=False,
    )
```

```python
import functools

import jax
import jax.numpy as jnp
import ml_dtypes
import numpy as np
from jax import lax
from jax.experimental import pallas as pl
from jax.experimental.pallas import tpu as pltpu
from jax.sharding import PartitionSpec as P

VMEM_BYTES = 56 * 1024 * 1024
PAD = 8
LANES = 128


def cosine_table(size):
    freq = np.arange(size, dtype=np.float64)[:, None]
    place = np.arange(size, dtype=np.float64)[None, :]
    waves = np.cos(np.pi * (2.0 * place + 1.0) * freq / (2.0 * size))
    scales = np.where(freq == 0.0, np.sqrt(1.0 / size), np.sqrt(2.0 / size))
    return (scales * waves).astype(ml_dtypes.bfloat16)


def weight_of(counts):
    values = counts.astype(jnp.float32)
    return values / (values + 4.0)


def strip_rows(rows):
    return 32 if rows % 32 == 0 else 8


def partner(index, step):
    return index ^ step


def device():
    return lax.axis_index("wide") * lax.axis_size("narrow") + lax.axis_index("narrow")


def planes_kernel(start, planes, total, block, sizes, normals, counts, lines, low, high, low_counts,
                  high_counts, table, *rest):
    *outs, flux_y, last_x, partial, divergence, ordered = rest
    step = pl.program_id(0)
    steps = planes // block
    rows, depth = last_x.shape
    strip = strip_rows(rows)
    strips = [slice(r, r + strip) for r in range(0, rows, strip)]
    columns = [slice(c, c + LANES) for c in range(0, depth, LANES)]
    now = lax.rem(step, 2)
    before = 1 - now
    here, narrow = lax.axis_index("narrow"), lines.shape[0]
    below = jnp.where(here > 0, here - 1, here)
    above = jnp.where(here < narrow - 1, here + 1, here)

    @pl.when(step == 0)
    def _():
        if sizes is None:
            ordered[...] = table[...]
        else:
            far, near = sizes
            slab = depth // (far * near)
            for place in range(near):
                for turn in range(far):
                    owner = partner(device() // near, turn) * near + partner(device() % near, place)
                    into = (place * far + turn) * slab
                    ordered[into:into + slab, :] = table[pl.ds(pl.multiple_of(owner * slab, slab), slab), :]
        for at in strips:
            if start == 0:
                last_x[at, :] = low[at, :].astype(jnp.float32)
            else:
                last_x[at, :] = weight_of(low_counts[0, at, :]) * low[0, 0, at, :].astype(jnp.float32)

    def transform(plane):
        along = lax.dot_general(
            ordered[...], divergence[plane], (((1,), (1,)), ((), ())), preferred_element_type=jnp.float32
        ).astype(jnp.bfloat16)
        share = depth // len(outs)
        for at, out in enumerate(outs):
            out[:, plane] = along[at * share:(at + 1) * share].reshape(out.shape[0], out.shape[2], rows)

    def diff_y(slot, plane, tile, at):
        after_y = flux_y[slot, plane, tile, PAD + at.start + 1:PAD + at.stop + 1, :]
        return after_y - flux_y[slot, plane, tile, PAD + at.start - 1:PAD + at.stop - 1, :]

    lane = lax.broadcasted_iota(jnp.int32, (strip, LANES), 1)
    first, last = lane == 0, lane == LANES - 1

    def take_in(at):
        ahead = []
        for plane in range(block):
            flux_x, before_z, after_z = [], [], []
            for tile, cut in enumerate(columns):
                weight = weight_of(counts[plane, at, cut])
                flux_x.append(weight * normals[0, plane, at, cut].astype(jnp.float32))
                flux_y[now, plane, tile, PAD + at.start:PAD + at.stop, :] = (
                    weight * normals[1, plane, at, cut].astype(jnp.float32)
                )
                flux_z = weight * normals[2, plane, at, cut].astype(jnp.float32)
                before_z.append(pltpu.roll(flux_z, 1, 1))
                after_z.append(pltpu.roll(flux_z, LANES - 1, 1))
            for tile, cut in enumerate(columns):
                left = before_z[tile - 1] if tile > 0 else 0.0
                right = after_z[tile + 1] if tile + 1 < len(columns) else 0.0
                diff_z = jnp.where(last, right, after_z[tile]) - jnp.where(first, left, before_z[tile])
                if plane == 0:
                    partial[block, at, cut] = partial[block - 1, at, cut] + flux_x[tile]
                    partial[0, at, cut] = diff_z - last_x[at, cut]
                else:
                    partial[plane - 1, at, cut] = partial[plane - 1, at, cut] + flux_x[tile]
                    partial[plane, at, cut] = diff_z - ahead[tile]
                if plane == block - 1:
                    last_x[at, cut] = flux_x[tile]
            ahead = flux_x

    def put_out(at):
        for tile, cut in enumerate(columns):
            done = partial[block, at, cut] + diff_y(before, block - 1, tile, at)
            divergence[block - 1, at, cut] = done.astype(jnp.bfloat16)
            for plane in range(block - 1):
                done = partial[plane, at, cut] + diff_y(now, plane, tile, at)
                divergence[plane, at, cut] = done.astype(jnp.bfloat16)

    @pl.when(step < steps)
    def _():
        for plane in range(block - 1):
            transform(plane)
        for plane in range(block):
            low_line = lines[below, pl.ds(start + step * block + plane, 1), :]
            high_line = lines[above, pl.ds(start + step * block + plane, 1), :]
            for tile, cut in enumerate(columns):
                flux_y[now, plane, tile, PAD - 1:PAD, :] = low_line[:, cut]
                flux_y[now, plane, tile, PAD + rows:PAD + rows + 1, :] = high_line[:, cut]
        for number, at in enumerate(strips):
            take_in(at)
            if number:
                put_out(strips[number - 1])
        put_out(strips[-1])
        transform(block - 1)

    @pl.when(step == steps)
    def _():
        for plane in range(block - 1):
            transform(plane)
        for at in strips:
            for tile, cut in enumerate(columns):
                if start + planes == total:
                    flux_x = high[at, cut].astype(jnp.float32)
                else:
                    flux_x = weight_of(high_counts[0, at, cut]) * high[0, 0, at, cut].astype(jnp.float32)
                done = flux_x + (partial[block - 1, at, cut] + diff_y(before, block - 1, tile, at))
                divergence[block - 1, at, cut] = done.astype(jnp.bfloat16)
        transform(block - 1)


def along_z_of(normals, counts, halos, table, start, planes, count=1, groups=1, sizes=None):
    _, total, rows, depth = normals.shape
    lines, low_x, high_x = halos
    block = 4 if planes % 4 == 0 else 1
    steps = planes // block

    def block_at(step):
        return start // block + jnp.minimum(step, steps - 1)

    def edge(plane):
        return pl.BlockSpec((1, 1, rows, depth), lambda step: (0, plane, 0, 0))

    def edge_counts(plane):
        return pl.BlockSpec((1, rows, depth), lambda step: (plane, 0, 0))

    whole = pl.BlockSpec((rows, depth), lambda step: (0, 0))
    at_low, at_high = start == 0, start + planes == total
    below, above = max(start - 1, 0), min(start + planes, total - 1)
    size = planes * rows * depth
    share = depth // (groups * count)
    return pl.pallas_call(
        functools.partial(planes_kernel, start, planes, total, block, sizes),
        grid=(steps + 1,),
        in_specs=[
            pl.BlockSpec((3, block, rows, depth), lambda step: (0, block_at(step), 0, 0)),
            pl.BlockSpec((block, rows, depth), lambda step: (block_at(step), 0, 0)),
            pl.BlockSpec(lines.shape, lambda step: (0, 0, 0)),
            whole if at_low else edge(below),
            whole if at_high else edge(above),
            edge_counts(below),
            edge_counts(above),
            pl.BlockSpec((depth, depth), lambda step: (0, 0)),
        ],
        out_specs=[
            pl.BlockSpec((groups, block, share, rows), lambda step: (0, jnp.maximum(step - 1, 0), 0, 0))
        ] * count,
        out_shape=[jax.ShapeDtypeStruct((groups, planes, share, rows), jnp.bfloat16)] * count,
        scratch_shapes=[
            pltpu.VMEM((2, block, depth // LANES, rows + 2 * PAD, LANES), jnp.float32),
            pltpu.VMEM((rows, depth), jnp.float32),
            pltpu.VMEM((block + 1, rows, depth), jnp.float32),
            pltpu.VMEM((block, rows, depth), jnp.bfloat16),
            pltpu.VMEM((depth, depth), jnp.bfloat16),
        ],
        compiler_params=pltpu.CompilerParams(vmem_limit_bytes=VMEM_BYTES),
        cost_estimate=pl.CostEstimate(flops=2 * size * depth, bytes_accessed=12 * size, transcendentals=size),
    )(normals, counts, lines, low_x if at_low else normals, high_x if at_high else normals, counts, counts, table)


def order_of(planes, slab):
    order = np.zeros((slab, planes, planes, slab), np.float32)
    for k in range(slab):
        for i in range(planes):
            order[k, i, i, k] = 1.0
    return jnp.asarray(order.reshape(planes * slab, planes * slab).astype(ml_dtypes.bfloat16))


def y_of(groups, table, order):
    planes, slab, rows = groups[0][0].shape
    count = planes * slab
    lines = [
        jnp.concatenate([tile[...].reshape(count, rows) for tile in tiles], axis=1) for tiles in groups
    ]
    along = jnp.dot(jnp.concatenate(lines, axis=0), table[...], preferred_element_type=jnp.float32)
    along = along.astype(jnp.bfloat16)
    moved = []
    for at in range(len(groups)):
        part = jnp.dot(order[...], along[at * count:(at + 1) * count], preferred_element_type=jnp.float32)
        moved.append(part.astype(jnp.bfloat16).reshape(slab, planes, table.shape[1]))
    return moved


def near_kernel(near, narrow, *refs):
    tiles, (table, order), (*outs, ordered) = refs[:near], refs[near:near + 2], refs[near + 2:]
    planes, _, rows = tiles[0].shape

    @pl.when(pl.program_id(0) == 0)
    def _():
        for place in range(narrow):
            owner = partner(device() % narrow, place)
            ordered[place * rows:(place + 1) * rows, :] = table[pl.ds(pl.multiple_of(owner * rows, rows), rows), :]

    moved = y_of([tiles[at:at + narrow] for at in range(0, near, narrow)], ordered, order)
    for step, out in enumerate(outs):

        @pl.when(pl.program_id(0) == step)
        def _():
            for core, part in enumerate(moved):
                out[:, core * planes:(core + 1) * planes, :] = part


def far_kernel(narrow, tiles, table, order, *rest):
    out = rest[-1]
    groups = [[tiles.at[at + place] for place in range(narrow)] for at in range(0, tiles.shape[0], narrow)]
    for at, moved in enumerate(y_of(groups, table, order)):
        out[:, at] = moved


def y_cost(planes, slab, wide, full_y):
    size = planes * slab * wide * full_y
    return pl.CostEstimate(flops=2 * size * (full_y + planes * slab), bytes_accessed=4 * size, transcendentals=0)


def along_y_near(tiles, table, far, narrow):
    planes, share, rows = tiles[0].shape
    near = len(tiles)
    slab = share // far
    full_y = table.shape[1]
    count = planes * slab
    cores = near // narrow
    return pl.pallas_call(
        functools.partial(near_kernel, near, narrow),
        grid=(far,),
        in_specs=[pl.BlockSpec((planes, slab, rows), lambda step: (0, step, 0))] * near + [
            pl.BlockSpec(table.shape, lambda step: (0, 0)),
            pl.BlockSpec((count, count), lambda step: (0, 0)),
        ],
        out_specs=[pl.BlockSpec((slab, cores * planes, full_y), lambda step: (0, 0, 0))] * far,
        out_shape=[jax.ShapeDtypeStruct((slab, cores * planes, full_y), jnp.bfloat16)] * far,
        scratch_shapes=[pltpu.VMEM(table.shape, jnp.bfloat16)],
        compiler_params=pltpu.CompilerParams(vmem_limit_bytes=VMEM_BYTES),
        cost_estimate=y_cost(planes, slab, far * cores, full_y),
    )(*tiles, table, order_of(planes, slab))


def along_y_far(tiles, table, so_far, start, total, narrow):
    count, planes, slab, rows = tiles.shape
    wide = count // narrow
    full_y = table.shape[1]
    group = max(1, 512 // (planes * slab))
    operands = [tiles, table, order_of(planes, slab)]
    in_specs = [
        pl.BlockSpec((group * narrow, planes, slab, rows), lambda at: (at, 0, 0, 0)),
        pl.BlockSpec(table.shape, lambda at: (0, 0)),
        pl.BlockSpec((planes * slab, planes * slab), lambda at: (0, 0)),
    ]
    aliases = {}
    if so_far is not None:
        operands.append(so_far.reshape(slab, wide, total, full_y))
        in_specs.append(pl.BlockSpec(memory_space=pl.ANY))
        aliases = {3: 0}
    return pl.pallas_call(
        functools.partial(far_kernel, narrow),
        grid=(wide // group,),
        in_specs=in_specs,
        out_specs=pl.BlockSpec((slab, group, planes, full_y), lambda at: (0, at, start // planes, 0)),
        out_shape=jax.ShapeDtypeStruct((slab, wide, total, full_y), jnp.bfloat16),
        input_output_aliases=aliases,
        compiler_params=pltpu.CompilerParams(vmem_limit_bytes=VMEM_BYTES),
        cost_estimate=y_cost(planes, slab, wide, full_y),
    )(*operands).reshape(slab, wide * total, full_y)


def after(array, *others):
    return lax.optimization_barrier((array, *others))[0]


def swap_far(array, step, near):
    if step == 0:
        return array
    count = lax.axis_size("wide") * lax.axis_size("narrow")
    pairs = [(i, partner(i // near, step) * near + i % near) for i in range(count)]
    return lax.ppermute(array, ("wide", "narrow"), pairs)


def swap_near(array, step, near):
    if step == 0:
        return array
    count = lax.axis_size("wide") * lax.axis_size("narrow")
    pairs = [(i, i // near * near + partner(i % near, step)) for i in range(count)]
    return lax.ppermute(array, ("wide", "narrow"), pairs)


def halos_of(normals, counts):
    wide = lax.axis_size("wide")
    narrow = lax.axis_size("narrow")
    here = lax.axis_index("narrow")
    edge_y = lambda at: weight_of(counts[:, at, :]) * normals[1, :, at, :].astype(jnp.float32)
    edge_x = lambda at: (weight_of(counts[at]) * normals[0, at].astype(jnp.float32)).astype(jnp.bfloat16)
    to = lax.broadcasted_iota(jnp.int32, (narrow, 1, 1), 0)
    lines = jnp.where(to == here + 1, edge_y(counts.shape[1] - 1), jnp.where(to == here - 1, edge_y(0), 0.0))
    lines = lax.all_to_all(lines, "narrow", split_axis=0, concat_axis=0, tiled=True)
    low_x = lax.ppermute(edge_x(counts.shape[0] - 1), "wide", [(i, i + 1) for i in range(wide - 1)])
    high_x = lax.ppermute(edge_x(0), "wide", [(i + 1, i) for i in range(wide - 1)])
    return lines, low_x, high_x


def per_device(normals, counts):
    wide = lax.axis_size("wide")
    narrow = lax.axis_size("narrow")
    _, total, rows, depth = normals.shape
    full_y = narrow * rows
    slab = depth // (wide * narrow)
    halos = halos_of(normals, counts)
    table_z = jnp.asarray(cosine_table(depth) * ml_dtypes.bfloat16(0.5))
    table_y = jnp.asarray(np.ascontiguousarray(cosine_table(full_y).T))
    cores = 2
    far = wide // cores
    near = cores * narrow
    if slab % 16 == 0 and total % 32 == 0 and wide == cores * far and far & (far - 1) == 0 and near & (near - 1) == 0:
        few = total // 4
        third, first, second = 0, few, 2 * few
        pieces = along_z_of(normals, counts, halos, table_z, first, few, 1, wide * narrow)[0]
        pieces = after(pieces, *halos)
        arrived = lax.all_to_all(pieces, ("wide", "narrow"), split_axis=0, concat_axis=0, tiled=True)
        later = after(table_z, pieces)
        tiles = along_z_of(normals, counts, halos, later, third, few, near, 1, (far, near))
        later = after(table_z, tiles[0])
        tiles = [swap_near(tile[0], step, near) for step, tile in enumerate(tiles)]
        pieces = along_z_of(normals, counts, halos, later, second, 2 * few, 1, wide * narrow)[0]
        arrived_later = lax.all_to_all(pieces, ("wide", "narrow"), split_axis=0, concat_axis=0, tiled=True)
        far_pieces = along_y_near(tiles, table_y, far, narrow)
        arrived = after(arrived, far_pieces[0])
        far_pieces = [swap_far(piece, step, near) for step, piece in enumerate(far_pieces)]
        spectrum = along_y_far(arrived, table_y, None, first, total, narrow)
        spectrum = along_y_far(arrived_later, table_y, spectrum, second, total, narrow)
        mine = device() // near
        for step, piece in enumerate(far_pieces):
            for turn in range(cores):
                core = partner(device() % near // narrow, turn)
                at = (partner(mine, step) * cores + core) * total + third
                spectrum = lax.dynamic_update_slice(spectrum, piece[:, turn * few:(turn + 1) * few], (0, at, 0))
        return spectrum
    along = along_z_of(normals, counts, halos, table_z, 0, total)[0]
    along = along.reshape(total, wide * narrow, slab, rows)
    arrived = lax.all_to_all(along, ("wide", "narrow"), split_axis=1, concat_axis=1, tiled=True)
    arrived = arrived.reshape(total, wide, narrow, slab, rows)
    pencil = jnp.transpose(arrived, (3, 1, 0, 2, 4)).reshape(slab * wide * total, full_y)
    spectrum = jnp.dot(pencil, table_y, preferred_element_type=jnp.float32).astype(jnp.bfloat16)
    return spectrum.reshape(slab, wide * total, full_y)


def solution(mesh):
    placed = (P(None, "wide", "narrow", None), P("wide", "narrow", None))
    return jax.shard_map(
        per_device,
        mesh=mesh,
        in_specs=placed,
        out_specs=P(("wide", "narrow"), None, None),
        check_vma=False,
    )
```

```python
import functools

import jax
import jax.numpy as jnp
import ml_dtypes
import numpy as np
from jax import lax
from jax.experimental import pallas as pl
from jax.experimental.pallas import tpu as pltpu
from jax.sharding import PartitionSpec as P

VMEM_BYTES = 56 * 1024 * 1024
PAD = 8
LANES = 128


def cosine_table(size):
    freq = np.arange(size, dtype=np.float64)[:, None]
    place = np.arange(size, dtype=np.float64)[None, :]
    waves = np.cos(np.pi * (2.0 * place + 1.0) * freq / (2.0 * size))
    scales = np.where(freq == 0.0, np.sqrt(1.0 / size), np.sqrt(2.0 / size))
    return (scales * waves).astype(ml_dtypes.bfloat16)


def weight_of(counts):
    values = counts.astype(jnp.float32)
    return values / (values + 4.0)


def strip_rows(rows):
    return 32 if rows % 32 == 0 else 8


def partner(index, step):
    return index ^ step


def device():
    return lax.axis_index("wide") * lax.axis_size("narrow") + lax.axis_index("narrow")


def planes_kernel(start, planes, total, block, sizes, normals, counts, lines, low, high, low_counts,
                  high_counts, table, *rest):
    *outs, flux_y, last_x, partial, divergence, ordered = rest
    step = pl.program_id(0)
    steps = planes // block
    rows, depth = last_x.shape
    strip = strip_rows(rows)
    strips = [slice(r, r + strip) for r in range(0, rows, strip)]
    columns = [slice(c, c + LANES) for c in range(0, depth, LANES)]
    now = lax.rem(step, 2)
    before = 1 - now
    here, narrow = lax.axis_index("narrow"), lines.shape[0]
    below = jnp.where(here > 0, here - 1, here)
    above = jnp.where(here < narrow - 1, here + 1, here)

    @pl.when(step == 0)
    def _():
        if sizes is None:
            ordered[...] = table[...]
        else:
            far, near = sizes
            slab = depth // (far * near)
            for place in range(near):
                for turn in range(far):
                    owner = partner(device() // near, turn) * near + partner(device() % near, place)
                    into = (place * far + turn) * slab
                    ordered[into:into + slab, :] = table[pl.ds(pl.multiple_of(owner * slab, slab), slab), :]
        for at in strips:
            if start == 0:
                last_x[at, :] = low[at, :].astype(jnp.float32)
            else:
                last_x[at, :] = weight_of(low_counts[0, at, :]) * low[0, 0, at, :].astype(jnp.float32)

    def transform(plane):
        along = lax.dot_general(
            ordered[...], divergence[plane], (((1,), (1,)), ((), ())), preferred_element_type=jnp.float32
        ).astype(jnp.bfloat16)
        share = depth // len(outs)
        for at, out in enumerate(outs):
            out[:, plane] = along[at * share:(at + 1) * share].reshape(out.shape[0], out.shape[2], rows)

    def diff_y(slot, plane, tile, at):
        after_y = flux_y[slot, plane, tile, PAD + at.start + 1:PAD + at.stop + 1, :]
        return after_y - flux_y[slot, plane, tile, PAD + at.start - 1:PAD + at.stop - 1, :]

    lane = lax.broadcasted_iota(jnp.int32, (strip, LANES), 1)
    first, last = lane == 0, lane == LANES - 1

    def take_in(at):
        ahead = []
        for plane in range(block):
            flux_x, before_z, after_z = [], [], []
            for tile, cut in enumerate(columns):
                weight = weight_of(counts[plane, at, cut])
                flux_x.append(weight * normals[0, plane, at, cut].astype(jnp.float32))
                flux_y[now, plane, tile, PAD + at.start:PAD + at.stop, :] = (
                    weight * normals[1, plane, at, cut].astype(jnp.float32)
                )
                flux_z = weight * normals[2, plane, at, cut].astype(jnp.float32)
                before_z.append(pltpu.roll(flux_z, 1, 1))
                after_z.append(pltpu.roll(flux_z, LANES - 1, 1))
            for tile, cut in enumerate(columns):
                left = before_z[tile - 1] if tile > 0 else 0.0
                right = after_z[tile + 1] if tile + 1 < len(columns) else 0.0
                diff_z = jnp.where(last, right, after_z[tile]) - jnp.where(first, left, before_z[tile])
                if plane == 0:
                    partial[block, at, cut] = partial[block - 1, at, cut] + flux_x[tile]
                    partial[0, at, cut] = diff_z - last_x[at, cut]
                else:
                    partial[plane - 1, at, cut] = partial[plane - 1, at, cut] + flux_x[tile]
                    partial[plane, at, cut] = diff_z - ahead[tile]
                if plane == block - 1:
                    last_x[at, cut] = flux_x[tile]
            ahead = flux_x

    def put_out(at):
        for tile, cut in enumerate(columns):
            done = partial[block, at, cut] + diff_y(before, block - 1, tile, at)
            divergence[block - 1, at, cut] = done.astype(jnp.bfloat16)
            for plane in range(block - 1):
                done = partial[plane, at, cut] + diff_y(now, plane, tile, at)
                divergence[plane, at, cut] = done.astype(jnp.bfloat16)

    @pl.when(step < steps)
    def _():
        for plane in range(block - 1):
            transform(plane)
        for plane in range(block):
            low_line = lines[below, pl.ds(start + step * block + plane, 1), :]
            high_line = lines[above, pl.ds(start + step * block + plane, 1), :]
            for tile, cut in enumerate(columns):
                flux_y[now, plane, tile, PAD - 1:PAD, :] = low_line[:, cut]
                flux_y[now, plane, tile, PAD + rows:PAD + rows + 1, :] = high_line[:, cut]
        for number, at in enumerate(strips):
            take_in(at)
            if number:
                put_out(strips[number - 1])
        put_out(strips[-1])
        transform(block - 1)

    @pl.when(step == steps)
    def _():
        for plane in range(block - 1):
            transform(plane)
        for at in strips:
            for tile, cut in enumerate(columns):
                if start + planes == total:
                    flux_x = high[at, cut].astype(jnp.float32)
                else:
                    flux_x = weight_of(high_counts[0, at, cut]) * high[0, 0, at, cut].astype(jnp.float32)
                done = flux_x + (partial[block - 1, at, cut] + diff_y(before, block - 1, tile, at))
                divergence[block - 1, at, cut] = done.astype(jnp.bfloat16)
        transform(block - 1)


def along_z_of(normals, counts, halos, table, start, planes, count=1, groups=1, sizes=None):
    _, total, rows, depth = normals.shape
    lines, low_x, high_x = halos
    block = 4 if planes % 4 == 0 else 1
    steps = planes // block

    def block_at(step):
        return start // block + jnp.minimum(step, steps - 1)

    def edge(plane):
        return pl.BlockSpec((1, 1, rows, depth), lambda step: (0, plane, 0, 0))

    def edge_counts(plane):
        return pl.BlockSpec((1, rows, depth), lambda step: (plane, 0, 0))

    whole = pl.BlockSpec((rows, depth), lambda step: (0, 0))
    at_low, at_high = start == 0, start + planes == total
    below, above = max(start - 1, 0), min(start + planes, total - 1)
    size = planes * rows * depth
    share = depth // (groups * count)
    return pl.pallas_call(
        functools.partial(planes_kernel, start, planes, total, block, sizes),
        grid=(steps + 1,),
        in_specs=[
            pl.BlockSpec((3, block, rows, depth), lambda step: (0, block_at(step), 0, 0)),
            pl.BlockSpec((block, rows, depth), lambda step: (block_at(step), 0, 0)),
            pl.BlockSpec(lines.shape, lambda step: (0, 0, 0)),
            whole if at_low else edge(below),
            whole if at_high else edge(above),
            edge_counts(below),
            edge_counts(above),
            pl.BlockSpec((depth, depth), lambda step: (0, 0)),
        ],
        out_specs=[
            pl.BlockSpec((groups, block, share, rows), lambda step: (0, jnp.maximum(step - 1, 0), 0, 0))
        ] * count,
        out_shape=[jax.ShapeDtypeStruct((groups, planes, share, rows), jnp.bfloat16)] * count,
        scratch_shapes=[
            pltpu.VMEM((2, block, depth // LANES, rows + 2 * PAD, LANES), jnp.float32),
            pltpu.VMEM((rows, depth), jnp.float32),
            pltpu.VMEM((block + 1, rows, depth), jnp.float32),
            pltpu.VMEM((block, rows, depth), jnp.bfloat16),
            pltpu.VMEM((depth, depth), jnp.bfloat16),
        ],
        compiler_params=pltpu.CompilerParams(vmem_limit_bytes=VMEM_BYTES),
        cost_estimate=pl.CostEstimate(flops=2 * size * depth, bytes_accessed=12 * size, transcendentals=size),
    )(normals, counts, lines, low_x if at_low else normals, high_x if at_high else normals, counts, counts, table)


def order_of(planes, slab):
    order = np.zeros((slab, planes, planes, slab), np.float32)
    for k in range(slab):
        for i in range(planes):
            order[k, i, i, k] = 1.0
    return jnp.asarray(order.reshape(planes * slab, planes * slab).astype(ml_dtypes.bfloat16))


def y_of(groups, table, order):
    planes, slab, rows = groups[0][0].shape
    count = planes * slab
    lines = [
        jnp.concatenate([tile[...].reshape(count, rows) for tile in tiles], axis=1) for tiles in groups
    ]
    along = jnp.dot(jnp.concatenate(lines, axis=0), table[...], preferred_element_type=jnp.float32)
    along = along.astype(jnp.bfloat16)
    moved = []
    for at in range(len(groups)):
        part = jnp.dot(order[...], along[at * count:(at + 1) * count], preferred_element_type=jnp.float32)
        moved.append(part.astype(jnp.bfloat16).reshape(slab, planes, table.shape[1]))
    return moved


def near_kernel(near, narrow, *refs):
    tiles, (table, order), (*outs, ordered) = refs[:near], refs[near:near + 2], refs[near + 2:]
    planes, _, rows = tiles[0].shape

    @pl.when(pl.program_id(0) == 0)
    def _():
        for place in range(narrow):
            owner = partner(device() % narrow, place)
            ordered[place * rows:(place + 1) * rows, :] = table[pl.ds(pl.multiple_of(owner * rows, rows), rows), :]

    moved = y_of([tiles[at:at + narrow] for at in range(0, near, narrow)], ordered, order)
    for step, out in enumerate(outs):

        @pl.when(pl.program_id(0) == step)
        def _():
            for core, part in enumerate(moved):
                out[:, core * planes:(core + 1) * planes, :] = part


def far_kernel(narrow, tiles, table, order, *rest):
    out = rest[-1]
    groups = [[tiles.at[at + place] for place in range(narrow)] for at in range(0, tiles.shape[0], narrow)]
    for at, moved in enumerate(y_of(groups, table, order)):
        out[:, at] = moved


def y_cost(planes, slab, wide, full_y):
    size = planes * slab * wide * full_y
    return pl.CostEstimate(flops=2 * size * (full_y + planes * slab), bytes_accessed=4 * size, transcendentals=0)


def along_y_near(tiles, table, far, narrow):
    planes, share, rows = tiles[0].shape
    near = len(tiles)
    slab = share // far
    full_y = table.shape[1]
    count = planes * slab
    cores = near // narrow
    return pl.pallas_call(
        functools.partial(near_kernel, near, narrow),
        grid=(far,),
        in_specs=[pl.BlockSpec((planes, slab, rows), lambda step: (0, step, 0))] * near + [
            pl.BlockSpec(table.shape, lambda step: (0, 0)),
            pl.BlockSpec((count, count), lambda step: (0, 0)),
        ],
        out_specs=[pl.BlockSpec((slab, cores * planes, full_y), lambda step: (0, 0, 0))] * far,
        out_shape=[jax.ShapeDtypeStruct((slab, cores * planes, full_y), jnp.bfloat16)] * far,
        scratch_shapes=[pltpu.VMEM(table.shape, jnp.bfloat16)],
        compiler_params=pltpu.CompilerParams(vmem_limit_bytes=VMEM_BYTES),
        cost_estimate=y_cost(planes, slab, far * cores, full_y),
    )(*tiles, table, order_of(planes, slab))


def along_y_far(tiles, table, so_far, start, total, narrow):
    count, planes, slab, rows = tiles.shape
    wide = count // narrow
    full_y = table.shape[1]
    group = max(1, 512 // (planes * slab))
    operands = [tiles, table, order_of(planes, slab)]
    in_specs = [
        pl.BlockSpec((group * narrow, planes, slab, rows), lambda at: (at, 0, 0, 0)),
        pl.BlockSpec(table.shape, lambda at: (0, 0)),
        pl.BlockSpec((planes * slab, planes * slab), lambda at: (0, 0)),
    ]
    aliases = {}
    if so_far is not None:
        operands.append(so_far.reshape(slab, wide, total, full_y))
        in_specs.append(pl.BlockSpec(memory_space=pl.ANY))
        aliases = {3: 0}
    return pl.pallas_call(
        functools.partial(far_kernel, narrow),
        grid=(wide // group,),
        in_specs=in_specs,
        out_specs=pl.BlockSpec((slab, group, planes, full_y), lambda at: (0, at, start // planes, 0)),
        out_shape=jax.ShapeDtypeStruct((slab, wide, total, full_y), jnp.bfloat16),
        input_output_aliases=aliases,
        compiler_params=pltpu.CompilerParams(vmem_limit_bytes=VMEM_BYTES),
        cost_estimate=y_cost(planes, slab, wide, full_y),
    )(*operands).reshape(slab, wide * total, full_y)


def after(array, *others):
    return lax.optimization_barrier((array, *others))[0]


def swap_far(array, step, near):
    if step == 0:
        return array
    count = lax.axis_size("wide") * lax.axis_size("narrow")
    pairs = [(i, partner(i // near, step) * near + i % near) for i in range(count)]
    return lax.ppermute(array, ("wide", "narrow"), pairs)


def swap_near(array, step, near):
    if step == 0:
        return array
    count = lax.axis_size("wide") * lax.axis_size("narrow")
    pairs = [(i, i // near * near + partner(i % near, step)) for i in range(count)]
    return lax.ppermute(array, ("wide", "narrow"), pairs)


def edges_kernel(low_y, high_y, low_y_counts, high_y_counts, low_x, high_x, low_x_counts, high_x_counts,
                 lines, low_plane, high_plane):
    narrow = lines.shape[0]
    here = lax.axis_index("narrow")
    last = low_y_counts.shape[1] - 1
    first_line = weight_of(low_y_counts[:, 0, :]) * low_y[0, :, 0, :].astype(jnp.float32)
    last_line = weight_of(high_y_counts[:, last, :]) * high_y[0, :, high_y.shape[2] - 1, :].astype(jnp.float32)
    for to in range(narrow):
        lines[to] = jnp.where(here + 1 == to, last_line, jnp.where(here - 1 == to, first_line, 0.0))
    low_plane[...] = (weight_of(low_x_counts[0]) * low_x[0, 0].astype(jnp.float32)).astype(jnp.bfloat16)
    high_plane[...] = (weight_of(high_x_counts[0]) * high_x[0, 0].astype(jnp.float32)).astype(jnp.bfloat16)


def edges_of(normals, counts, narrow):
    _, total, rows, depth = normals.shape
    few, fewer = 16, 8
    whole = pl.BlockSpec((rows, depth), lambda at: (0, 0))
    return pl.pallas_call(
        edges_kernel,
        grid=(1,),
        in_specs=[
            pl.BlockSpec((1, total, few, depth), lambda at: (1, 0, 0, 0)),
            pl.BlockSpec((1, total, few, depth), lambda at: (1, 0, rows // few - 1, 0)),
            pl.BlockSpec((total, fewer, depth), lambda at: (0, 0, 0)),
            pl.BlockSpec((total, fewer, depth), lambda at: (0, rows // fewer - 1, 0)),
            pl.BlockSpec((1, 1, rows, depth), lambda at: (0, 0, 0, 0)),
            pl.BlockSpec((1, 1, rows, depth), lambda at: (0, total - 1, 0, 0)),
            pl.BlockSpec((1, rows, depth), lambda at: (0, 0, 0)),
            pl.BlockSpec((1, rows, depth), lambda at: (total - 1, 0, 0)),
        ],
        out_specs=[pl.BlockSpec((narrow, total, depth), lambda at: (0, 0, 0)), whole, whole],
        out_shape=[
            jax.ShapeDtypeStruct((narrow, total, depth), jnp.float32),
            jax.ShapeDtypeStruct((rows, depth), jnp.bfloat16),
            jax.ShapeDtypeStruct((rows, depth), jnp.bfloat16),
        ],
        compiler_params=pltpu.CompilerParams(vmem_limit_bytes=VMEM_BYTES),
    )(normals, normals, counts, counts, normals, normals, counts, counts)


def halos_of(normals, counts):
    wide = lax.axis_size("wide")
    lines, first, last = edges_of(normals, counts, lax.axis_size("narrow"))
    lines = lax.all_to_all(lines, "narrow", split_axis=0, concat_axis=0, tiled=True)
    low_x = lax.ppermute(last, "wide", [(i, i + 1) for i in range(wide - 1)])
    high_x = lax.ppermute(first, "wide", [(i + 1, i) for i in range(wide - 1)])
    return lines, low_x, high_x


def per_device(normals, counts):
    wide = lax.axis_size("wide")
    narrow = lax.axis_size("narrow")
    _, total, rows, depth = normals.shape
    full_y = narrow * rows
    slab = depth // (wide * narrow)
    halos = halos_of(normals, counts)
    table_z = jnp.asarray(cosine_table(depth) * ml_dtypes.bfloat16(0.5))
    table_y = jnp.asarray(np.ascontiguousarray(cosine_table(full_y).T))
    cores = 2
    far = wide // cores
    near = cores * narrow
    if slab % 16 == 0 and total % 32 == 0 and wide == cores * far and far & (far - 1) == 0 and near & (near - 1) == 0:
        few = total // 4
        third, first, second = 0, few, 2 * few
        pieces = along_z_of(normals, counts, halos, table_z, first, few, 1, wide * narrow)[0]
        pieces = after(pieces, *halos)
        arrived = lax.all_to_all(pieces, ("wide", "narrow"), split_axis=0, concat_axis=0, tiled=True)
        later = after(table_z, pieces)
        tiles = along_z_of(normals, counts, halos, later, third, few, near, 1, (far, near))
        later = after(table_z, tiles[0])
        tiles = [swap_near(tile[0], step, near) for step, tile in enumerate(tiles)]
        pieces = along_z_of(normals, counts, halos, later, second, 2 * few, 1, wide * narrow)[0]
        arrived_later = lax.all_to_all(pieces, ("wide", "narrow"), split_axis=0, concat_axis=0, tiled=True)
        far_pieces = along_y_near(tiles, table_y, far, narrow)
        arrived = after(arrived, far_pieces[0])
        far_pieces = [swap_far(piece, step, near) for step, piece in enumerate(far_pieces)]
        spectrum = along_y_far(arrived, table_y, None, first, total, narrow)
        spectrum = along_y_far(arrived_later, table_y, spectrum, second, total, narrow)
        mine = device() // near
        for step, piece in enumerate(far_pieces):
            for turn in range(cores):
                core = partner(device() % near // narrow, turn)
                at = (partner(mine, step) * cores + core) * total + third
                spectrum = lax.dynamic_update_slice(spectrum, piece[:, turn * few:(turn + 1) * few], (0, at, 0))
        return spectrum
    along = along_z_of(normals, counts, halos, table_z, 0, total)[0]
    along = along.reshape(total, wide * narrow, slab, rows)
    arrived = lax.all_to_all(along, ("wide", "narrow"), split_axis=1, concat_axis=1, tiled=True)
    arrived = arrived.reshape(total, wide, narrow, slab, rows)
    pencil = jnp.transpose(arrived, (3, 1, 0, 2, 4)).reshape(slab * wide * total, full_y)
    spectrum = jnp.dot(pencil, table_y, preferred_element_type=jnp.float32).astype(jnp.bfloat16)
    return spectrum.reshape(slab, wide * total, full_y)


def solution(mesh):
    placed = (P(None, "wide", "narrow", None), P("wide", "narrow", None))
    return jax.shard_map(
        per_device,
        mesh=mesh,
        in_specs=placed,
        out_specs=P(("wide", "narrow"), None, None),
        check_vma=False,
    )
```

```python
import functools

import jax
import jax.numpy as jnp
import ml_dtypes
import numpy as np
from jax import lax
from jax.experimental import pallas as pl
from jax.experimental.pallas import tpu as pltpu
from jax.sharding import PartitionSpec as P

VMEM_BYTES = 56 * 1024 * 1024
PAD = 8
LANES = 128


def cosine_table(size):
    freq = np.arange(size, dtype=np.float64)[:, None]
    place = np.arange(size, dtype=np.float64)[None, :]
    waves = np.cos(np.pi * (2.0 * place + 1.0) * freq / (2.0 * size))
    scales = np.where(freq == 0.0, np.sqrt(1.0 / size), np.sqrt(2.0 / size))
    return (scales * waves).astype(ml_dtypes.bfloat16)


def weight_of(counts):
    values = counts.astype(jnp.float32)
    return values / (values + 4.0)


def strip_rows(rows):
    return 32 if rows % 32 == 0 else 8


def partner(index, step):
    return index ^ step


def device():
    return lax.axis_index("wide") * lax.axis_size("narrow") + lax.axis_index("narrow")


def planes_kernel(start, planes, total, block, sizes, normals, counts, lines, low, high, low_counts,
                  high_counts, table, *rest):
    *outs, flux_y, last_x, partial, divergence, ordered = rest
    step = pl.program_id(0)
    steps = planes // block
    rows, depth = last_x.shape
    strip = strip_rows(rows)
    strips = [slice(r, r + strip) for r in range(0, rows, strip)]
    columns = [slice(c, c + LANES) for c in range(0, depth, LANES)]
    now = lax.rem(step, 2)
    before = 1 - now
    here, narrow = lax.axis_index("narrow"), lines.shape[0]
    below = jnp.where(here > 0, here - 1, here)
    above = jnp.where(here < narrow - 1, here + 1, here)

    @pl.when(step == 0)
    def _():
        if sizes is None:
            ordered[...] = table[...]
        else:
            far, near = sizes
            slab = depth // (far * near)
            for place in range(near):
                for turn in range(far):
                    owner = partner(device() // near, turn) * near + partner(device() % near, place)
                    into = (place * far + turn) * slab
                    ordered[into:into + slab, :] = table[pl.ds(pl.multiple_of(owner * slab, slab), slab), :]
        for at in strips:
            if start == 0:
                last_x[at, :] = low[at, :].astype(jnp.float32)
            else:
                last_x[at, :] = weight_of(low_counts[0, at, :]) * low[0, 0, at, :].astype(jnp.float32)

    def transform(plane):
        along = lax.dot_general(
            ordered[...], divergence[plane], (((1,), (1,)), ((), ())), preferred_element_type=jnp.float32
        ).astype(jnp.bfloat16)
        share = depth // len(outs)
        for at, out in enumerate(outs):
            out[:, plane] = along[at * share:(at + 1) * share].reshape(out.shape[0], out.shape[2], rows)

    def diff_y(slot, plane, tile, at):
        after_y = flux_y[slot, plane, tile, PAD + at.start + 1:PAD + at.stop + 1, :]
        return after_y - flux_y[slot, plane, tile, PAD + at.start - 1:PAD + at.stop - 1, :]

    lane = lax.broadcasted_iota(jnp.int32, (strip, LANES), 1)
    first, last = lane == 0, lane == LANES - 1

    def take_in(at):
        ahead = []
        for plane in range(block):
            flux_x, before_z, after_z = [], [], []
            for tile, cut in enumerate(columns):
                weight = weight_of(counts[plane, at, cut])
                flux_x.append(weight * normals[0, plane, at, cut].astype(jnp.float32))
                flux_y[now, plane, tile, PAD + at.start:PAD + at.stop, :] = (
                    weight * normals[1, plane, at, cut].astype(jnp.float32)
                )
                flux_z = weight * normals[2, plane, at, cut].astype(jnp.float32)
                before_z.append(pltpu.roll(flux_z, 1, 1))
                after_z.append(pltpu.roll(flux_z, LANES - 1, 1))
            for tile, cut in enumerate(columns):
                left = before_z[tile - 1] if tile > 0 else 0.0
                right = after_z[tile + 1] if tile + 1 < len(columns) else 0.0
                diff_z = jnp.where(last, right, after_z[tile]) - jnp.where(first, left, before_z[tile])
                if plane == 0:
                    partial[block, at, cut] = partial[block - 1, at, cut] + flux_x[tile]
                    partial[0, at, cut] = diff_z - last_x[at, cut]
                else:
                    partial[plane - 1, at, cut] = partial[plane - 1, at, cut] + flux_x[tile]
                    partial[plane, at, cut] = diff_z - ahead[tile]
                if plane == block - 1:
                    last_x[at, cut] = flux_x[tile]
            ahead = flux_x

    def put_out(at):
        for tile, cut in enumerate(columns):
            done = partial[block, at, cut] + diff_y(before, block - 1, tile, at)
            divergence[block - 1, at, cut] = done.astype(jnp.bfloat16)
            for plane in range(block - 1):
                done = partial[plane, at, cut] + diff_y(now, plane, tile, at)
                divergence[plane, at, cut] = done.astype(jnp.bfloat16)

    @pl.when(step < steps)
    def _():
        for plane in range(block - 1):
            transform(plane)
        for plane in range(block):
            low_line = lines[below, pl.ds(start + step * block + plane, 1), :]
            high_line = lines[above, pl.ds(start + step * block + plane, 1), :]
            for tile, cut in enumerate(columns):
                flux_y[now, plane, tile, PAD - 1:PAD, :] = low_line[:, cut]
                flux_y[now, plane, tile, PAD + rows:PAD + rows + 1, :] = high_line[:, cut]
        for number, at in enumerate(strips):
            take_in(at)
            if number:
                put_out(strips[number - 1])
        put_out(strips[-1])
        transform(block - 1)

    @pl.when(step == steps)
    def _():
        for plane in range(block - 1):
            transform(plane)
        for at in strips:
            for tile, cut in enumerate(columns):
                if start + planes == total:
                    flux_x = high[at, cut].astype(jnp.float32)
                else:
                    flux_x = weight_of(high_counts[0, at, cut]) * high[0, 0, at, cut].astype(jnp.float32)
                done = flux_x + (partial[block - 1, at, cut] + diff_y(before, block - 1, tile, at))
                divergence[block - 1, at, cut] = done.astype(jnp.bfloat16)
        transform(block - 1)


def along_z_of(normals, counts, halos, table, start, planes, count=1, groups=1, sizes=None):
    _, total, rows, depth = normals.shape
    lines, low_x, high_x = halos
    block = 4 if planes % 4 == 0 else 1
    steps = planes // block

    def block_at(step):
        return start // block + jnp.minimum(step, steps - 1)

    def edge(plane):
        return pl.BlockSpec((1, 1, rows, depth), lambda step: (0, plane, 0, 0))

    def edge_counts(plane):
        return pl.BlockSpec((1, rows, depth), lambda step: (plane, 0, 0))

    whole = pl.BlockSpec((rows, depth), lambda step: (0, 0))
    at_low, at_high = start == 0, start + planes == total
    below, above = max(start - 1, 0), min(start + planes, total - 1)
    size = planes * rows * depth
    share = depth // (groups * count)
    return pl.pallas_call(
        functools.partial(planes_kernel, start, planes, total, block, sizes),
        grid=(steps + 1,),
        in_specs=[
            pl.BlockSpec((3, block, rows, depth), lambda step: (0, block_at(step), 0, 0)),
            pl.BlockSpec((block, rows, depth), lambda step: (block_at(step), 0, 0)),
            pl.BlockSpec(lines.shape, lambda step: (0, 0, 0)),
            whole if at_low else edge(below),
            whole if at_high else edge(above),
            edge_counts(below),
            edge_counts(above),
            pl.BlockSpec((depth, depth), lambda step: (0, 0)),
        ],
        out_specs=[
            pl.BlockSpec((groups, block, share, rows), lambda step: (0, jnp.maximum(step - 1, 0), 0, 0))
        ] * count,
        out_shape=[jax.ShapeDtypeStruct((groups, planes, share, rows), jnp.bfloat16)] * count,
        scratch_shapes=[
            pltpu.VMEM((2, block, depth // LANES, rows + 2 * PAD, LANES), jnp.float32),
            pltpu.VMEM((rows, depth), jnp.float32),
            pltpu.VMEM((block + 1, rows, depth), jnp.float32),
            pltpu.VMEM((block, rows, depth), jnp.bfloat16),
            pltpu.VMEM((depth, depth), jnp.bfloat16),
        ],
        compiler_params=pltpu.CompilerParams(vmem_limit_bytes=VMEM_BYTES),
        cost_estimate=pl.CostEstimate(flops=2 * size * depth, bytes_accessed=12 * size, transcendentals=size),
    )(normals, counts, lines, low_x if at_low else normals, high_x if at_high else normals, counts, counts, table)


def order_of(planes, slab):
    order = np.zeros((slab, planes, planes, slab), np.float32)
    for k in range(slab):
        for i in range(planes):
            order[k, i, i, k] = 1.0
    return jnp.asarray(order.reshape(planes * slab, planes * slab).astype(ml_dtypes.bfloat16))


def y_of(groups, table, order):
    planes, slab, rows = groups[0][0].shape
    count = planes * slab
    lines = [
        jnp.concatenate([tile[...].reshape(count, rows) for tile in tiles], axis=1) for tiles in groups
    ]
    along = jnp.dot(jnp.concatenate(lines, axis=0), table[...], preferred_element_type=jnp.float32)
    along = along.astype(jnp.bfloat16)
    moved = []
    for at in range(len(groups)):
        part = jnp.dot(order[...], along[at * count:(at + 1) * count], preferred_element_type=jnp.float32)
        moved.append(part.astype(jnp.bfloat16).reshape(slab, planes, table.shape[1]))
    return moved


def pick(parts, chosen):
    picked = parts[0]
    for part, here in zip(parts[1:], chosen[1:]):
        picked = jnp.where(here, part, picked)
    return picked


def near_kernel(near, narrow, *refs):
    tiles, (table, order), (*outs, ordered) = refs[:near], refs[near:near + 2], refs[near + 2:]
    planes, _, rows = tiles[0].shape

    @pl.when(pl.program_id(0) == 0)
    def _():
        for place in range(narrow):
            owner = partner(device() % narrow, place)
            ordered[place * rows:(place + 1) * rows, :] = table[pl.ds(pl.multiple_of(owner * rows, rows), rows), :]

    moved = y_of([tiles[at:at + narrow] for at in range(0, near, narrow)], ordered, order)
    own = device() % near // narrow
    moved = [pick(moved, [own == partner(turn, core) for turn in range(len(moved))]) for core in range(len(moved))]
    for step, out in enumerate(outs):

        @pl.when(pl.program_id(0) == step)
        def _():
            for core, part in enumerate(moved):
                out[:, core] = part


def far_kernel(narrow, tiles, table, order, *rest):
    out = rest[-1]
    groups = [[tiles.at[at + place] for place in range(narrow)] for at in range(0, tiles.shape[0], narrow)]
    for at, moved in enumerate(y_of(groups, table, order)):
        out[:, at] = moved


def y_cost(planes, slab, wide, full_y):
    size = planes * slab * wide * full_y
    return pl.CostEstimate(flops=2 * size * (full_y + planes * slab), bytes_accessed=4 * size, transcendentals=0)


def along_y_near(tiles, table, far, narrow):
    planes, share, rows = tiles[0].shape
    near = len(tiles)
    slab = share // far
    full_y = table.shape[1]
    count = planes * slab
    cores = near // narrow
    return pl.pallas_call(
        functools.partial(near_kernel, near, narrow),
        grid=(far,),
        in_specs=[pl.BlockSpec((planes, slab, rows), lambda step: (0, step, 0))] * near + [
            pl.BlockSpec(table.shape, lambda step: (0, 0)),
            pl.BlockSpec((count, count), lambda step: (0, 0)),
        ],
        out_specs=[pl.BlockSpec((slab, cores, planes, full_y), lambda step: (0, 0, 0, 0))] * far,
        out_shape=[jax.ShapeDtypeStruct((slab, cores, planes, full_y), jnp.bfloat16)] * far,
        scratch_shapes=[pltpu.VMEM(table.shape, jnp.bfloat16)],
        compiler_params=pltpu.CompilerParams(vmem_limit_bytes=VMEM_BYTES),
        cost_estimate=y_cost(planes, slab, far * cores, full_y),
    )(*tiles, table, order_of(planes, slab))


def along_y_far(tiles, table, so_far, start, total, narrow):
    count, planes, slab, rows = tiles.shape
    wide = count // narrow
    full_y = table.shape[1]
    group = max(1, 512 // (planes * slab))
    operands = [tiles, table, order_of(planes, slab)]
    in_specs = [
        pl.BlockSpec((group * narrow, planes, slab, rows), lambda at: (at, 0, 0, 0)),
        pl.BlockSpec(table.shape, lambda at: (0, 0)),
        pl.BlockSpec((planes * slab, planes * slab), lambda at: (0, 0)),
    ]
    aliases = {}
    if so_far is not None:
        operands.append(so_far.reshape(slab, wide, total, full_y))
        in_specs.append(pl.BlockSpec(memory_space=pl.ANY))
        aliases = {3: 0}
    return pl.pallas_call(
        functools.partial(far_kernel, narrow),
        grid=(wide // group,),
        in_specs=in_specs,
        out_specs=pl.BlockSpec((slab, group, planes, full_y), lambda at: (0, at, start // planes, 0)),
        out_shape=jax.ShapeDtypeStruct((slab, wide, total, full_y), jnp.bfloat16),
        input_output_aliases=aliases,
        compiler_params=pltpu.CompilerParams(vmem_limit_bytes=VMEM_BYTES),
        cost_estimate=y_cost(planes, slab, wide, full_y),
    )(*operands).reshape(slab, wide * total, full_y)


def after(array, *others):
    return lax.optimization_barrier((array, *others))[0]


def swap_far(array, step, near):
    if step == 0:
        return array
    count = lax.axis_size("wide") * lax.axis_size("narrow")
    pairs = [(i, partner(i // near, step) * near + i % near) for i in range(count)]
    return lax.ppermute(array, ("wide", "narrow"), pairs)


def swap_near(array, step, near):
    if step == 0:
        return array
    count = lax.axis_size("wide") * lax.axis_size("narrow")
    pairs = [(i, i // near * near + partner(i % near, step)) for i in range(count)]
    return lax.ppermute(array, ("wide", "narrow"), pairs)


def edges_kernel(low_y, high_y, low_y_counts, high_y_counts, low_x, high_x, low_x_counts, high_x_counts,
                 lines, low_plane, high_plane):
    narrow = lines.shape[0]
    here = lax.axis_index("narrow")
    last = low_y_counts.shape[1] - 1
    first_line = weight_of(low_y_counts[:, 0, :]) * low_y[0, :, 0, :].astype(jnp.float32)
    last_line = weight_of(high_y_counts[:, last, :]) * high_y[0, :, high_y.shape[2] - 1, :].astype(jnp.float32)
    for to in range(narrow):
        lines[to] = jnp.where(here + 1 == to, last_line, jnp.where(here - 1 == to, first_line, 0.0))
    low_plane[...] = (weight_of(low_x_counts[0]) * low_x[0, 0].astype(jnp.float32)).astype(jnp.bfloat16)
    high_plane[...] = (weight_of(high_x_counts[0]) * high_x[0, 0].astype(jnp.float32)).astype(jnp.bfloat16)


def edges_of(normals, counts, narrow):
    _, total, rows, depth = normals.shape
    few, fewer = 16, 8
    whole = pl.BlockSpec((rows, depth), lambda at: (0, 0))
    return pl.pallas_call(
        edges_kernel,
        grid=(1,),
        in_specs=[
            pl.BlockSpec((1, total, few, depth), lambda at: (1, 0, 0, 0)),
            pl.BlockSpec((1, total, few, depth), lambda at: (1, 0, rows // few - 1, 0)),
            pl.BlockSpec((total, fewer, depth), lambda at: (0, 0, 0)),
            pl.BlockSpec((total, fewer, depth), lambda at: (0, rows // fewer - 1, 0)),
            pl.BlockSpec((1, 1, rows, depth), lambda at: (0, 0, 0, 0)),
            pl.BlockSpec((1, 1, rows, depth), lambda at: (0, total - 1, 0, 0)),
            pl.BlockSpec((1, rows, depth), lambda at: (0, 0, 0)),
            pl.BlockSpec((1, rows, depth), lambda at: (total - 1, 0, 0)),
        ],
        out_specs=[pl.BlockSpec((narrow, total, depth), lambda at: (0, 0, 0)), whole, whole],
        out_shape=[
            jax.ShapeDtypeStruct((narrow, total, depth), jnp.float32),
            jax.ShapeDtypeStruct((rows, depth), jnp.bfloat16),
            jax.ShapeDtypeStruct((rows, depth), jnp.bfloat16),
        ],
        compiler_params=pltpu.CompilerParams(vmem_limit_bytes=VMEM_BYTES),
    )(normals, normals, counts, counts, normals, normals, counts, counts)


def halos_of(normals, counts):
    wide = lax.axis_size("wide")
    lines, first, last = edges_of(normals, counts, lax.axis_size("narrow"))
    lines = lax.all_to_all(lines, "narrow", split_axis=0, concat_axis=0, tiled=True)
    low_x = lax.ppermute(last, "wide", [(i, i + 1) for i in range(wide - 1)])
    high_x = lax.ppermute(first, "wide", [(i + 1, i) for i in range(wide - 1)])
    return lines, low_x, high_x


def per_device(normals, counts):
    wide = lax.axis_size("wide")
    narrow = lax.axis_size("narrow")
    _, total, rows, depth = normals.shape
    full_y = narrow * rows
    slab = depth // (wide * narrow)
    halos = halos_of(normals, counts)
    table_z = jnp.asarray(cosine_table(depth) * ml_dtypes.bfloat16(0.5))
    table_y = jnp.asarray(np.ascontiguousarray(cosine_table(full_y).T))
    cores = 2
    far = wide // cores
    near = cores * narrow
    if slab % 16 == 0 and total % 32 == 0 and wide == cores * far and far & (far - 1) == 0 and near & (near - 1) == 0:
        few = total // 4
        third, first, second = 0, few, 2 * few
        pieces = along_z_of(normals, counts, halos, table_z, first, few, 1, wide * narrow)[0]
        pieces = after(pieces, *halos)
        arrived = lax.all_to_all(pieces, ("wide", "narrow"), split_axis=0, concat_axis=0, tiled=True)
        later = after(table_z, pieces)
        tiles = along_z_of(normals, counts, halos, later, third, few, near, 1, (far, near))
        later = after(table_z, tiles[0])
        tiles = [swap_near(tile[0], step, near) for step, tile in enumerate(tiles)]
        pieces = along_z_of(normals, counts, halos, later, second, 2 * few, 1, wide * narrow)[0]
        arrived_later = lax.all_to_all(pieces, ("wide", "narrow"), split_axis=0, concat_axis=0, tiled=True)
        far_pieces = along_y_near(tiles, table_y, far, narrow)
        arrived = after(arrived, far_pieces[0])
        far_pieces = [swap_far(piece, step, near) for step, piece in enumerate(far_pieces)]
        spectrum = along_y_far(arrived, table_y, None, first, total, narrow)
        spectrum = along_y_far(arrived_later, table_y, spectrum, second, total, narrow)
        spectrum = spectrum.reshape(slab, wide, total, full_y)
        for step, piece in enumerate(far_pieces):
            at = partner(device() // near, step) * cores
            spectrum = lax.dynamic_update_slice(spectrum, piece, (0, at, third, 0))
        return spectrum.reshape(slab, wide * total, full_y)
    along = along_z_of(normals, counts, halos, table_z, 0, total)[0]
    along = along.reshape(total, wide * narrow, slab, rows)
    arrived = lax.all_to_all(along, ("wide", "narrow"), split_axis=1, concat_axis=1, tiled=True)
    arrived = arrived.reshape(total, wide, narrow, slab, rows)
    pencil = jnp.transpose(arrived, (3, 1, 0, 2, 4)).reshape(slab * wide * total, full_y)
    spectrum = jnp.dot(pencil, table_y, preferred_element_type=jnp.float32).astype(jnp.bfloat16)
    return spectrum.reshape(slab, wide * total, full_y)


def solution(mesh):
    placed = (P(None, "wide", "narrow", None), P("wide", "narrow", None))
    return jax.shard_map(
        per_device,
        mesh=mesh,
        in_specs=placed,
        out_specs=P(("wide", "narrow"), None, None),
        check_vma=False,
    )
```

```python
import functools

import jax
import jax.numpy as jnp
import ml_dtypes
import numpy as np
from jax import lax
from jax.experimental import pallas as pl
from jax.experimental.pallas import tpu as pltpu
from jax.sharding import PartitionSpec as P

VMEM_BYTES = 56 * 1024 * 1024
PAD = 8
LANES = 128


def cosine_table(size):
    freq = np.arange(size, dtype=np.float64)[:, None]
    place = np.arange(size, dtype=np.float64)[None, :]
    waves = np.cos(np.pi * (2.0 * place + 1.0) * freq / (2.0 * size))
    scales = np.where(freq == 0.0, np.sqrt(1.0 / size), np.sqrt(2.0 / size))
    return (scales * waves).astype(ml_dtypes.bfloat16)


def weight_of(counts):
    values = counts.astype(jnp.float32)
    return values / (values + 4.0)


def strip_rows(rows):
    return 32 if rows % 32 == 0 else 8


def partner(index, step):
    return index ^ step


def device():
    return lax.axis_index("wide") * lax.axis_size("narrow") + lax.axis_index("narrow")


def planes_kernel(start, planes, total, block, sizes, normals, counts, lines, low, high, low_counts,
                  high_counts, table, *rest):
    *outs, flux_y, last_x, partial, divergence, ordered = rest
    step = pl.program_id(0)
    steps = planes // block
    rows, depth = last_x.shape
    strip = strip_rows(rows)
    strips = [slice(r, r + strip) for r in range(0, rows, strip)]
    columns = [slice(c, c + LANES) for c in range(0, depth, LANES)]
    now = lax.rem(step, 2)
    before = 1 - now
    here, narrow = lax.axis_index("narrow"), lines.shape[0]
    below = jnp.where(here > 0, here - 1, here)
    above = jnp.where(here < narrow - 1, here + 1, here)

    @pl.when(step == 0)
    def _():
        if sizes is None:
            ordered[...] = table[...]
        else:
            far, near = sizes
            slab = depth // (far * near)
            for place in range(near):
                for turn in range(far):
                    owner = partner(device() // near, turn) * near + partner(device() % near, place)
                    into = (place * far + turn) * slab
                    ordered[into:into + slab, :] = table[pl.ds(pl.multiple_of(owner * slab, slab), slab), :]
        for at in strips:
            if start == 0:
                last_x[at, :] = low[at, :].astype(jnp.float32)
            else:
                last_x[at, :] = weight_of(low_counts[0, at, :]) * low[0, 0, at, :].astype(jnp.float32)

    def transform(plane):
        along = lax.dot_general(
            ordered[...], divergence[plane], (((1,), (1,)), ((), ())), preferred_element_type=jnp.float32
        ).astype(jnp.bfloat16)
        share = depth // len(outs)
        for at, out in enumerate(outs):
            out[:, plane] = along[at * share:(at + 1) * share].reshape(out.shape[0], out.shape[2], rows)

    def diff_y(slot, plane, tile, at):
        after_y = flux_y[slot, plane, tile, PAD + at.start + 1:PAD + at.stop + 1, :]
        return after_y - flux_y[slot, plane, tile, PAD + at.start - 1:PAD + at.stop - 1, :]

    lane = lax.broadcasted_iota(jnp.int32, (strip, LANES), 1)
    first, last = lane == 0, lane == LANES - 1

    def take_in(at):
        ahead = []
        for plane in range(block):
            flux_x, before_z, after_z = [], [], []
            for tile, cut in enumerate(columns):
                weight = weight_of(counts[plane, at, cut])
                flux_x.append(weight * normals[0, plane, at, cut].astype(jnp.float32))
                flux_y[now, plane, tile, PAD + at.start:PAD + at.stop, :] = (
                    weight * normals[1, plane, at, cut].astype(jnp.float32)
                )
                flux_z = weight * normals[2, plane, at, cut].astype(jnp.float32)
                before_z.append(pltpu.roll(flux_z, 1, 1))
                after_z.append(pltpu.roll(flux_z, LANES - 1, 1))
            for tile, cut in enumerate(columns):
                left = before_z[tile - 1] if tile > 0 else 0.0
                right = after_z[tile + 1] if tile + 1 < len(columns) else 0.0
                diff_z = jnp.where(last, right, after_z[tile]) - jnp.where(first, left, before_z[tile])
                if plane == 0:
                    partial[block, at, cut] = partial[block - 1, at, cut] + flux_x[tile]
                    partial[0, at, cut] = diff_z - last_x[at, cut]
                else:
                    partial[plane - 1, at, cut] = partial[plane - 1, at, cut] + flux_x[tile]
                    partial[plane, at, cut] = diff_z - ahead[tile]
                if plane == block - 1:
                    last_x[at, cut] = flux_x[tile]
            ahead = flux_x

    def put_out(at):
        for tile, cut in enumerate(columns):
            done = partial[block, at, cut] + diff_y(before, block - 1, tile, at)
            divergence[block - 1, at, cut] = done.astype(jnp.bfloat16)
            for plane in range(block - 1):
                done = partial[plane, at, cut] + diff_y(now, plane, tile, at)
                divergence[plane, at, cut] = done.astype(jnp.bfloat16)

    @pl.when(step < steps)
    def _():
        for plane in range(block - 1):
            transform(plane)
        for plane in range(block):
            low_line = lines[below, pl.ds(start + step * block + plane, 1), :]
            high_line = lines[above, pl.ds(start + step * block + plane, 1), :]
            for tile, cut in enumerate(columns):
                flux_y[now, plane, tile, PAD - 1:PAD, :] = low_line[:, cut]
                flux_y[now, plane, tile, PAD + rows:PAD + rows + 1, :] = high_line[:, cut]
        for number, at in enumerate(strips):
            take_in(at)
            if number:
                put_out(strips[number - 1])
        put_out(strips[-1])
        transform(block - 1)

    @pl.when(step == steps)
    def _():
        for plane in range(block - 1):
            transform(plane)
        for at in strips:
            for tile, cut in enumerate(columns):
                if start + planes == total:
                    flux_x = high[at, cut].astype(jnp.float32)
                else:
                    flux_x = weight_of(high_counts[0, at, cut]) * high[0, 0, at, cut].astype(jnp.float32)
                done = flux_x + (partial[block - 1, at, cut] + diff_y(before, block - 1, tile, at))
                divergence[block - 1, at, cut] = done.astype(jnp.bfloat16)
        transform(block - 1)


def along_z_of(normals, counts, halos, table, start, planes, count=1, groups=1, sizes=None):
    _, total, rows, depth = normals.shape
    lines, low_x, high_x = halos
    block = 4 if planes % 4 == 0 else 1
    if planes == 4:
        block = 2
    steps = planes // block

    def block_at(step):
        return start // block + jnp.minimum(step, steps - 1)

    def edge(plane):
        return pl.BlockSpec((1, 1, rows, depth), lambda step: (0, plane, 0, 0))

    def edge_counts(plane):
        return pl.BlockSpec((1, rows, depth), lambda step: (plane, 0, 0))

    whole = pl.BlockSpec((rows, depth), lambda step: (0, 0))
    at_low, at_high = start == 0, start + planes == total
    below, above = max(start - 1, 0), min(start + planes, total - 1)
    size = (planes + 6) * rows * depth
    share = depth // (groups * count)
    return pl.pallas_call(
        functools.partial(planes_kernel, start, planes, total, block, sizes),
        grid=(steps + 1,),
        in_specs=[
            pl.BlockSpec((3, block, rows, depth), lambda step: (0, block_at(step), 0, 0)),
            pl.BlockSpec((block, rows, depth), lambda step: (block_at(step), 0, 0)),
            pl.BlockSpec(lines.shape, lambda step: (0, 0, 0)),
            whole if at_low else edge(below),
            whole if at_high else edge(above),
            edge_counts(below),
            edge_counts(above),
            pl.BlockSpec((depth, depth), lambda step: (0, 0)),
        ],
        out_specs=[
            pl.BlockSpec((groups, block, share, rows), lambda step: (0, jnp.maximum(step - 1, 0), 0, 0))
        ] * count,
        out_shape=[jax.ShapeDtypeStruct((groups, planes, share, rows), jnp.bfloat16)] * count,
        scratch_shapes=[
            pltpu.VMEM((2, block, depth // LANES, rows + 2 * PAD, LANES), jnp.float32),
            pltpu.VMEM((rows, depth), jnp.float32),
            pltpu.VMEM((block + 1, rows, depth), jnp.float32),
            pltpu.VMEM((block, rows, depth), jnp.bfloat16),
            pltpu.VMEM((depth, depth), jnp.bfloat16),
        ],
        compiler_params=pltpu.CompilerParams(vmem_limit_bytes=VMEM_BYTES),
        cost_estimate=pl.CostEstimate(flops=2 * size * depth, bytes_accessed=12 * size, transcendentals=size),
    )(normals, counts, lines, low_x if at_low else normals, high_x if at_high else normals, counts, counts, table)


def order_of(planes, slab):
    order = np.zeros((slab, planes, planes, slab), np.float32)
    for k in range(slab):
        for i in range(planes):
            order[k, i, i, k] = 1.0
    return jnp.asarray(order.reshape(planes * slab, planes * slab).astype(ml_dtypes.bfloat16))


def y_of(groups, table, order):
    slab, rows = groups[0][0][0].shape[1:]
    count = order.shape[0]
    lines = []
    for tiles in groups:
        columns = [
            jnp.concatenate([part[...].reshape(part.shape[0] * slab, rows) for part in tile], axis=0) for tile in tiles
        ]
        lines.append(jnp.concatenate(columns, axis=1))
    along = jnp.dot(jnp.concatenate(lines, axis=0), table[...], preferred_element_type=jnp.float32)
    along = along.astype(jnp.bfloat16)
    moved = []
    for at in range(len(groups)):
        part = jnp.dot(order[...], along[at * count:(at + 1) * count], preferred_element_type=jnp.float32)
        moved.append(part.astype(jnp.bfloat16).reshape(slab, count // slab, table.shape[1]))
    return moved


def pick(parts, chosen):
    picked = parts[0]
    for part, here in zip(parts[1:], chosen[1:]):
        picked = jnp.where(here, part, picked)
    return picked


def near_kernel(near, narrow, *refs):
    tiles, (table, order), (*outs, ordered) = refs[:near], refs[near:near + 2], refs[near + 2:]
    planes, _, rows = tiles[0].shape

    @pl.when(pl.program_id(0) == 0)
    def _():
        for place in range(narrow):
            owner = partner(device() % narrow, place)
            ordered[place * rows:(place + 1) * rows, :] = table[pl.ds(pl.multiple_of(owner * rows, rows), rows), :]

    moved = y_of([[[tile] for tile in tiles[at:at + narrow]] for at in range(0, near, narrow)], ordered, order)
    own = device() % near // narrow
    moved = [pick(moved, [own == partner(turn, core) for turn in range(len(moved))]) for core in range(len(moved))]
    for step, out in enumerate(outs):

        @pl.when(pl.program_id(0) == step)
        def _():
            for core, part in enumerate(moved):
                out[:, core] = part


def far_kernel(narrow, parts, *refs):
    tiles, (table, order, out) = refs[:parts], refs[parts:]
    groups = [
        [[part.at[at + place] for part in tiles] for place in range(narrow)]
        for at in range(0, tiles[0].shape[0], narrow)
    ]
    for at, moved in enumerate(y_of(groups, table, order)):
        out[:, at] = moved


def y_cost(planes, slab, wide, full_y):
    size = planes * slab * wide * full_y
    return pl.CostEstimate(flops=2 * size * (full_y + planes * slab), bytes_accessed=4 * size, transcendentals=0)


def along_y_near(tiles, table, far, narrow):
    planes, share, rows = tiles[0].shape
    near = len(tiles)
    slab = share // far
    full_y = table.shape[1]
    count = planes * slab
    cores = near // narrow
    return pl.pallas_call(
        functools.partial(near_kernel, near, narrow),
        grid=(far,),
        in_specs=[pl.BlockSpec((planes, slab, rows), lambda step: (0, step, 0))] * near + [
            pl.BlockSpec(table.shape, lambda step: (0, 0)),
            pl.BlockSpec((count, count), lambda step: (0, 0)),
        ],
        out_specs=[pl.BlockSpec((slab, cores, planes, full_y), lambda step: (0, 0, 0, 0))] * far,
        out_shape=[jax.ShapeDtypeStruct((slab, cores, planes, full_y), jnp.bfloat16)] * far,
        scratch_shapes=[pltpu.VMEM(table.shape, jnp.bfloat16)],
        compiler_params=pltpu.CompilerParams(vmem_limit_bytes=VMEM_BYTES),
        cost_estimate=y_cost(planes, slab, far * cores, full_y),
    )(*tiles, table, order_of(planes, slab))


def along_y_far(parts, table, total, narrow):
    count, _, slab, rows = parts[0].shape
    planes = sum(part.shape[1] for part in parts)
    wide = count // narrow
    full_y = table.shape[1]
    group = 2 if wide % 2 == 0 else 1
    return pl.pallas_call(
        functools.partial(far_kernel, narrow, len(parts)),
        grid=(wide // group,),
        in_specs=[
            pl.BlockSpec((group * narrow, part.shape[1], slab, rows), lambda at: (at, 0, 0, 0)) for part in parts
        ] + [
            pl.BlockSpec(table.shape, lambda at: (0, 0)),
            pl.BlockSpec((planes * slab, planes * slab), lambda at: (0, 0)),
        ],
        out_specs=pl.BlockSpec((slab, group, planes, full_y), lambda at: (0, at, 0, 0)),
        out_shape=jax.ShapeDtypeStruct((slab, wide, total, full_y), jnp.bfloat16),
        compiler_params=pltpu.CompilerParams(vmem_limit_bytes=VMEM_BYTES),
        cost_estimate=y_cost(planes, slab, wide, full_y),
    )(*parts, table, order_of(planes, slab))


def after(array, *others):
    return lax.optimization_barrier((array, *others))[0]


def swap_far(array, step, near):
    if step == 0:
        return array
    count = lax.axis_size("wide") * lax.axis_size("narrow")
    pairs = [(i, partner(i // near, step) * near + i % near) for i in range(count)]
    return lax.ppermute(array, ("wide", "narrow"), pairs)


def swap_near(array, step, near):
    if step == 0:
        return array
    count = lax.axis_size("wide") * lax.axis_size("narrow")
    pairs = [(i, i // near * near + partner(i % near, step)) for i in range(count)]
    return lax.ppermute(array, ("wide", "narrow"), pairs)


def edges_kernel(low_y, high_y, low_y_counts, high_y_counts, low_x, high_x, low_x_counts, high_x_counts,
                 lines, low_plane, high_plane):
    narrow = lines.shape[0]
    here = lax.axis_index("narrow")
    last = low_y_counts.shape[1] - 1
    first_line = weight_of(low_y_counts[:, 0, :]) * low_y[0, :, 0, :].astype(jnp.float32)
    last_line = weight_of(high_y_counts[:, last, :]) * high_y[0, :, high_y.shape[2] - 1, :].astype(jnp.float32)
    for to in range(narrow):
        lines[to] = jnp.where(here + 1 == to, last_line, jnp.where(here - 1 == to, first_line, 0.0))
    low_plane[...] = (weight_of(low_x_counts[0]) * low_x[0, 0].astype(jnp.float32)).astype(jnp.bfloat16)
    high_plane[...] = (weight_of(high_x_counts[0]) * high_x[0, 0].astype(jnp.float32)).astype(jnp.bfloat16)


def edges_of(normals, counts, narrow):
    _, total, rows, depth = normals.shape
    few, fewer = 16, 8
    whole = pl.BlockSpec((rows, depth), lambda at: (0, 0))
    return pl.pallas_call(
        edges_kernel,
        grid=(1,),
        in_specs=[
            pl.BlockSpec((1, total, few, depth), lambda at: (1, 0, 0, 0)),
            pl.BlockSpec((1, total, few, depth), lambda at: (1, 0, rows // few - 1, 0)),
            pl.BlockSpec((total, fewer, depth), lambda at: (0, 0, 0)),
            pl.BlockSpec((total, fewer, depth), lambda at: (0, rows // fewer - 1, 0)),
            pl.BlockSpec((1, 1, rows, depth), lambda at: (0, 0, 0, 0)),
            pl.BlockSpec((1, 1, rows, depth), lambda at: (0, total - 1, 0, 0)),
            pl.BlockSpec((1, rows, depth), lambda at: (0, 0, 0)),
            pl.BlockSpec((1, rows, depth), lambda at: (total - 1, 0, 0)),
        ],
        out_specs=[pl.BlockSpec((narrow, total, depth), lambda at: (0, 0, 0)), whole, whole],
        out_shape=[
            jax.ShapeDtypeStruct((narrow, total, depth), jnp.float32),
            jax.ShapeDtypeStruct((rows, depth), jnp.bfloat16),
            jax.ShapeDtypeStruct((rows, depth), jnp.bfloat16),
        ],
        compiler_params=pltpu.CompilerParams(vmem_limit_bytes=VMEM_BYTES),
    )(normals, normals, counts, counts, normals, normals, counts, counts)


def halos_of(normals, counts):
    wide = lax.axis_size("wide")
    lines, first, last = edges_of(normals, counts, lax.axis_size("narrow"))
    lines = lax.all_to_all(lines, "narrow", split_axis=0, concat_axis=0, tiled=True)
    low_x = lax.ppermute(last, "wide", [(i, i + 1) for i in range(wide - 1)])
    high_x = lax.ppermute(first, "wide", [(i + 1, i) for i in range(wide - 1)])
    return lines, low_x, high_x


def per_device(normals, counts):
    wide = lax.axis_size("wide")
    narrow = lax.axis_size("narrow")
    _, total, rows, depth = normals.shape
    full_y = narrow * rows
    slab = depth // (wide * narrow)
    halos = halos_of(normals, counts)
    table_z = jnp.asarray(cosine_table(depth) * ml_dtypes.bfloat16(0.5))
    table_y = jnp.asarray(np.ascontiguousarray(cosine_table(full_y).T))
    cores = 2
    far = wide // cores
    near = cores * narrow
    if slab % 16 == 0 and total % 32 == 0 and wide == cores * far and far & (far - 1) == 0 and near & (near - 1) == 0:
        few = total // 4
        fewer = few // 2
        third = 3 * few
        first, second = third - fewer, 0
        pieces = along_z_of(normals, counts, halos, table_z, first, fewer, 1, wide * narrow)[0]
        pieces = after(pieces, *halos)
        first_pieces = pieces
        arrived = lax.all_to_all(pieces, ("wide", "narrow"), split_axis=0, concat_axis=0, tiled=True)
        later = after(table_z, pieces)
        pieces = along_z_of(normals, counts, halos, later, second, first, 1, wide * narrow)[0]
        pieces = after(pieces, arrived)
        arrived_later = lax.all_to_all(pieces, ("wide", "narrow"), split_axis=0, concat_axis=0, tiled=True)
        later = after(table_z, first_pieces)
        tiles = along_z_of(normals, counts, halos, later, third, few, near, 1, (far, near))
        tiles = [swap_near(tile[0], step, near) for step, tile in enumerate(tiles)]
        far_pieces = along_y_near(tiles, table_y, far, narrow)
        far_pieces = [swap_far(piece, step, near) for step, piece in enumerate(far_pieces)]
        spectrum = along_y_far([after(arrived_later, far_pieces[0]), arrived], table_y, total, narrow)
        for step, piece in enumerate(far_pieces):
            at = partner(device() // near, step) * cores
            spectrum = lax.dynamic_update_slice(spectrum, piece, (0, at, third, 0))
        return spectrum.reshape(slab, wide * total, full_y)
    along = along_z_of(normals, counts, halos, table_z, 0, total)[0]
    along = along.reshape(total, wide * narrow, slab, rows)
    arrived = lax.all_to_all(along, ("wide", "narrow"), split_axis=1, concat_axis=1, tiled=True)
    arrived = arrived.reshape(total, wide, narrow, slab, rows)
    pencil = jnp.transpose(arrived, (3, 1, 0, 2, 4)).reshape(slab * wide * total, full_y)
    spectrum = jnp.dot(pencil, table_y, preferred_element_type=jnp.float32).astype(jnp.bfloat16)
    return spectrum.reshape(slab, wide * total, full_y)


def solution(mesh):
    placed = (P(None, "wide", "narrow", None), P("wide", "narrow", None))
    return jax.shard_map(
        per_device,
        mesh=mesh,
        in_specs=placed,
        out_specs=P(("wide", "narrow"), None, None),
        check_vma=False,
    )
```

```python
import functools

import jax
import jax.numpy as jnp
import ml_dtypes
import numpy as np
from jax import lax
from jax.experimental import pallas as pl
from jax.experimental.pallas import tpu as pltpu
from jax.sharding import PartitionSpec as P

VMEM_BYTES = 56 * 1024 * 1024
PAD = 8
LANES = 128


def cosine_table(size):
    freq = np.arange(size, dtype=np.float64)[:, None]
    place = np.arange(size, dtype=np.float64)[None, :]
    waves = np.cos(np.pi * (2.0 * place + 1.0) * freq / (2.0 * size))
    scales = np.where(freq == 0.0, np.sqrt(1.0 / size), np.sqrt(2.0 / size))
    return (scales * waves).astype(ml_dtypes.bfloat16)


def weight_of(counts):
    values = counts.astype(jnp.float32)
    return values / (values + 4.0)


def strip_rows(rows):
    return 32 if rows % 32 == 0 else 8


def partner(index, step):
    return index ^ step


def device():
    return lax.axis_index("wide") * lax.axis_size("narrow") + lax.axis_index("narrow")


def planes_kernel(start, planes, total, block, sizes, normals, counts, lines, low, high, low_counts,
                  high_counts, table, *rest):
    *outs, flux_y, last_x, partial, divergence, ordered = rest
    step = pl.program_id(0)
    steps = planes // block
    rows, depth = last_x.shape
    strip = strip_rows(rows)
    strips = [slice(r, r + strip) for r in range(0, rows, strip)]
    columns = [slice(c, c + LANES) for c in range(0, depth, LANES)]
    now = lax.rem(step, 2)
    before = 1 - now
    here, narrow = lax.axis_index("narrow"), lines.shape[0]
    below = jnp.where(here > 0, here - 1, here)
    above = jnp.where(here < narrow - 1, here + 1, here)

    @pl.when(step == 0)
    def _():
        if sizes is None:
            ordered[...] = table[...]
        else:
            far, near = sizes
            slab = depth // (far * near)
            for place in range(near):
                for turn in range(far):
                    owner = partner(device() // near, turn) * near + partner(device() % near, place)
                    into = (place * far + turn) * slab
                    ordered[into:into + slab, :] = table[pl.ds(pl.multiple_of(owner * slab, slab), slab), :]
        for at in strips:
            if start == 0:
                last_x[at, :] = low[at, :].astype(jnp.float32)
            else:
                last_x[at, :] = weight_of(low_counts[0, at, :]) * low[0, 0, at, :].astype(jnp.float32)

    def transform(plane):
        along = lax.dot_general(
            ordered[...], divergence[plane], (((1,), (1,)), ((), ())), preferred_element_type=jnp.float32
        ).astype(jnp.bfloat16)
        share = depth // len(outs)
        for at, out in enumerate(outs):
            out[:, plane] = along[at * share:(at + 1) * share].reshape(out.shape[0], out.shape[2], rows)

    def diff_y(slot, plane, tile, at):
        after_y = flux_y[slot, plane, tile, PAD + at.start + 1:PAD + at.stop + 1, :]
        return after_y - flux_y[slot, plane, tile, PAD + at.start - 1:PAD + at.stop - 1, :]

    lane = lax.broadcasted_iota(jnp.int32, (strip, LANES), 1)
    first, last = lane == 0, lane == LANES - 1

    def take_in(at):
        ahead = []
        for plane in range(block):
            flux_x, before_z, after_z = [], [], []
            for tile, cut in enumerate(columns):
                weight = weight_of(counts[plane, at, cut])
                flux_x.append(weight * normals[0, plane, at, cut].astype(jnp.float32))
                flux_y[now, plane, tile, PAD + at.start:PAD + at.stop, :] = (
                    weight * normals[1, plane, at, cut].astype(jnp.float32)
                )
                flux_z = weight * normals[2, plane, at, cut].astype(jnp.float32)
                before_z.append(pltpu.roll(flux_z, 1, 1))
                after_z.append(pltpu.roll(flux_z, LANES - 1, 1))
            for tile, cut in enumerate(columns):
                left = before_z[tile - 1] if tile > 0 else 0.0
                right = after_z[tile + 1] if tile + 1 < len(columns) else 0.0
                diff_z = jnp.where(last, right, after_z[tile]) - jnp.where(first, left, before_z[tile])
                if plane == 0:
                    partial[block, at, cut] = partial[block - 1, at, cut] + flux_x[tile]
                    partial[0, at, cut] = diff_z - last_x[at, cut]
                else:
                    partial[plane - 1, at, cut] = partial[plane - 1, at, cut] + flux_x[tile]
                    partial[plane, at, cut] = diff_z - ahead[tile]
                if plane == block - 1:
                    last_x[at, cut] = flux_x[tile]
            ahead = flux_x

    def put_out(at):
        for tile, cut in enumerate(columns):
            done = partial[block, at, cut] + diff_y(before, block - 1, tile, at)
            divergence[block - 1, at, cut] = done.astype(jnp.bfloat16)
            for plane in range(block - 1):
                done = partial[plane, at, cut] + diff_y(now, plane, tile, at)
                divergence[plane, at, cut] = done.astype(jnp.bfloat16)

    def go_on(begun):
        if begun:
            for plane in range(block - 1):
                transform(plane)
        for plane in range(block):
            low_line = lines[below, pl.ds(start + step * block + plane, 1), :]
            high_line = lines[above, pl.ds(start + step * block + plane, 1), :]
            for tile, cut in enumerate(columns):
                flux_y[now, plane, tile, PAD - 1:PAD, :] = low_line[:, cut]
                flux_y[now, plane, tile, PAD + rows:PAD + rows + 1, :] = high_line[:, cut]
        for number, at in enumerate(strips):
            take_in(at)
            if number:
                put_out(strips[number - 1])
        put_out(strips[-1])
        if begun:
            transform(block - 1)

    pl.when(step == 0)(lambda: go_on(False))
    pl.when(jnp.logical_and(step > 0, step < steps))(lambda: go_on(True))

    @pl.when(step == steps)
    def _():
        for plane in range(block - 1):
            transform(plane)
        for at in strips:
            for tile, cut in enumerate(columns):
                if start + planes == total:
                    flux_x = high[at, cut].astype(jnp.float32)
                else:
                    flux_x = weight_of(high_counts[0, at, cut]) * high[0, 0, at, cut].astype(jnp.float32)
                done = flux_x + (partial[block - 1, at, cut] + diff_y(before, block - 1, tile, at))
                divergence[block - 1, at, cut] = done.astype(jnp.bfloat16)
        transform(block - 1)


def along_z_of(normals, counts, halos, table, start, planes, count=1, groups=1, sizes=None):
    _, total, rows, depth = normals.shape
    lines, low_x, high_x = halos
    block = 4 if planes % 4 == 0 else 1
    if planes == 4:
        block = 2
    steps = planes // block

    def block_at(step):
        return start // block + jnp.minimum(step, steps - 1)

    def edge(plane):
        return pl.BlockSpec((1, 1, rows, depth), lambda step: (0, plane, 0, 0))

    def edge_counts(plane):
        return pl.BlockSpec((1, rows, depth), lambda step: (plane, 0, 0))

    whole = pl.BlockSpec((rows, depth), lambda step: (0, 0))
    at_low, at_high = start == 0, start + planes == total
    below, above = max(start - 1, 0), min(start + planes, total - 1)
    size = (planes + 6) * rows * depth
    share = depth // (groups * count)
    return pl.pallas_call(
        functools.partial(planes_kernel, start, planes, total, block, sizes),
        grid=(steps + 1,),
        in_specs=[
            pl.BlockSpec((3, block, rows, depth), lambda step: (0, block_at(step), 0, 0)),
            pl.BlockSpec((block, rows, depth), lambda step: (block_at(step), 0, 0)),
            pl.BlockSpec(lines.shape, lambda step: (0, 0, 0)),
            whole if at_low else edge(below),
            whole if at_high else edge(above),
            edge_counts(below),
            edge_counts(above),
            pl.BlockSpec((depth, depth), lambda step: (0, 0)),
        ],
        out_specs=[
            pl.BlockSpec((groups, block, share, rows), lambda step: (0, jnp.maximum(step - 1, 0), 0, 0))
        ] * count,
        out_shape=[jax.ShapeDtypeStruct((groups, planes, share, rows), jnp.bfloat16)] * count,
        scratch_shapes=[
            pltpu.VMEM((2, block, depth // LANES, rows + 2 * PAD, LANES), jnp.float32),
            pltpu.VMEM((rows, depth), jnp.float32),
            pltpu.VMEM((block + 1, rows, depth), jnp.float32),
            pltpu.VMEM((block, rows, depth), jnp.bfloat16),
            pltpu.VMEM((depth, depth), jnp.bfloat16),
        ],
        compiler_params=pltpu.CompilerParams(vmem_limit_bytes=VMEM_BYTES),
        cost_estimate=pl.CostEstimate(flops=2 * size * depth, bytes_accessed=12 * size, transcendentals=size),
    )(normals, counts, lines, low_x if at_low else normals, high_x if at_high else normals, counts, counts, table)


def order_of(planes, slab):
    order = np.zeros((slab, planes, planes, slab), np.float32)
    for k in range(slab):
        for i in range(planes):
            order[k, i, i, k] = 1.0
    return jnp.asarray(order.reshape(planes * slab, planes * slab).astype(ml_dtypes.bfloat16))


def y_of(groups, table, order):
    slab, rows = groups[0][0][0].shape[1:]
    count = order.shape[0]
    lines = []
    for tiles in groups:
        columns = [
            jnp.concatenate([part[...].reshape(part.shape[0] * slab, rows) for part in tile], axis=0) for tile in tiles
        ]
        lines.append(jnp.concatenate(columns, axis=1))
    along = jnp.dot(jnp.concatenate(lines, axis=0), table[...], preferred_element_type=jnp.float32)
    along = along.astype(jnp.bfloat16)
    moved = []
    for at in range(len(groups)):
        part = jnp.dot(order[...], along[at * count:(at + 1) * count], preferred_element_type=jnp.float32)
        moved.append(part.astype(jnp.bfloat16).reshape(slab, count // slab, table.shape[1]))
    return moved


def pick(parts, chosen):
    picked = parts[0]
    for part, here in zip(parts[1:], chosen[1:]):
        picked = jnp.where(here, part, picked)
    return picked


def near_kernel(near, narrow, *refs):
    tiles, (table, order), (*outs, ordered) = refs[:near], refs[near:near + 2], refs[near + 2:]
    planes, _, rows = tiles[0].shape

    @pl.when(pl.program_id(0) == 0)
    def _():
        for place in range(narrow):
            owner = partner(device() % narrow, place)
            ordered[place * rows:(place + 1) * rows, :] = table[pl.ds(pl.multiple_of(owner * rows, rows), rows), :]

    moved = y_of([[[tile] for tile in tiles[at:at + narrow]] for at in range(0, near, narrow)], ordered, order)
    own = device() % near // narrow
    moved = [pick(moved, [own == partner(turn, core) for turn in range(len(moved))]) for core in range(len(moved))]
    for step, out in enumerate(outs):

        @pl.when(pl.program_id(0) == step)
        def _():
            for core, part in enumerate(moved):
                out[:, core] = part


def far_kernel(narrow, parts, *refs):
    tiles, (table, order, out) = refs[:parts], refs[parts:]
    groups = [
        [[part.at[at + place] for part in tiles] for place in range(narrow)]
        for at in range(0, tiles[0].shape[0], narrow)
    ]
    for at, moved in enumerate(y_of(groups, table, order)):
        out[:, at] = moved


def y_cost(planes, slab, wide, full_y):
    size = planes * slab * wide * full_y
    return pl.CostEstimate(flops=2 * size * (full_y + planes * slab), bytes_accessed=4 * size, transcendentals=0)


def along_y_near(tiles, table, far, narrow):
    planes, share, rows = tiles[0].shape
    near = len(tiles)
    slab = share // far
    full_y = table.shape[1]
    count = planes * slab
    cores = near // narrow
    return pl.pallas_call(
        functools.partial(near_kernel, near, narrow),
        grid=(far,),
        in_specs=[pl.BlockSpec((planes, slab, rows), lambda step: (0, step, 0))] * near + [
            pl.BlockSpec(table.shape, lambda step: (0, 0)),
            pl.BlockSpec((count, count), lambda step: (0, 0)),
        ],
        out_specs=[pl.BlockSpec((slab, cores, planes, full_y), lambda step: (0, 0, 0, 0))] * far,
        out_shape=[jax.ShapeDtypeStruct((slab, cores, planes, full_y), jnp.bfloat16)] * far,
        scratch_shapes=[pltpu.VMEM(table.shape, jnp.bfloat16)],
        compiler_params=pltpu.CompilerParams(vmem_limit_bytes=VMEM_BYTES),
        cost_estimate=y_cost(planes, slab, far * cores, full_y),
    )(*tiles, table, order_of(planes, slab))


def along_y_far(parts, table, total, narrow):
    count, _, slab, rows = parts[0].shape
    planes = sum(part.shape[1] for part in parts)
    wide = count // narrow
    full_y = table.shape[1]
    group = 2 if wide % 2 == 0 else 1
    return pl.pallas_call(
        functools.partial(far_kernel, narrow, len(parts)),
        grid=(wide // group,),
        in_specs=[
            pl.BlockSpec((group * narrow, part.shape[1], slab, rows), lambda at: (at, 0, 0, 0)) for part in parts
        ] + [
            pl.BlockSpec(table.shape, lambda at: (0, 0)),
            pl.BlockSpec((planes * slab, planes * slab), lambda at: (0, 0)),
        ],
        out_specs=pl.BlockSpec((slab, group, planes, full_y), lambda at: (0, at, 0, 0)),
        out_shape=jax.ShapeDtypeStruct((slab, wide, total, full_y), jnp.bfloat16),
        compiler_params=pltpu.CompilerParams(vmem_limit_bytes=VMEM_BYTES),
        cost_estimate=y_cost(planes, slab, wide, full_y),
    )(*parts, table, order_of(planes, slab))


def after(array, *others):
    return lax.optimization_barrier((array, *others))[0]


def swap_far(array, step, near):
    if step == 0:
        return array
    count = lax.axis_size("wide") * lax.axis_size("narrow")
    pairs = [(i, partner(i // near, step) * near + i % near) for i in range(count)]
    return lax.ppermute(array, ("wide", "narrow"), pairs)


def swap_near(array, step, near):
    if step == 0:
        return array
    count = lax.axis_size("wide") * lax.axis_size("narrow")
    pairs = [(i, i // near * near + partner(i % near, step)) for i in range(count)]
    return lax.ppermute(array, ("wide", "narrow"), pairs)


def edges_kernel(low_y, high_y, low_y_counts, high_y_counts, low_x, high_x, low_x_counts, high_x_counts,
                 lines, low_plane, high_plane):
    narrow = lines.shape[0]
    here = lax.axis_index("narrow")
    last = low_y_counts.shape[1] - 1
    first_line = weight_of(low_y_counts[:, 0, :]) * low_y[0, :, 0, :].astype(jnp.float32)
    last_line = weight_of(high_y_counts[:, last, :]) * high_y[0, :, high_y.shape[2] - 1, :].astype(jnp.float32)
    for to in range(narrow):
        lines[to] = jnp.where(here + 1 == to, last_line, jnp.where(here - 1 == to, first_line, 0.0))
    low_plane[...] = (weight_of(low_x_counts[0]) * low_x[0, 0].astype(jnp.float32)).astype(jnp.bfloat16)
    high_plane[...] = (weight_of(high_x_counts[0]) * high_x[0, 0].astype(jnp.float32)).astype(jnp.bfloat16)


def edges_of(normals, counts, narrow):
    _, total, rows, depth = normals.shape
    few, fewer = 16, 8
    whole = pl.BlockSpec((rows, depth), lambda at: (0, 0))
    return pl.pallas_call(
        edges_kernel,
        grid=(1,),
        in_specs=[
            pl.BlockSpec((1, total, few, depth), lambda at: (1, 0, 0, 0)),
            pl.BlockSpec((1, total, few, depth), lambda at: (1, 0, rows // few - 1, 0)),
            pl.BlockSpec((total, fewer, depth), lambda at: (0, 0, 0)),
            pl.BlockSpec((total, fewer, depth), lambda at: (0, rows // fewer - 1, 0)),
            pl.BlockSpec((1, 1, rows, depth), lambda at: (0, 0, 0, 0)),
            pl.BlockSpec((1, 1, rows, depth), lambda at: (0, total - 1, 0, 0)),
            pl.BlockSpec((1, rows, depth), lambda at: (0, 0, 0)),
            pl.BlockSpec((1, rows, depth), lambda at: (total - 1, 0, 0)),
        ],
        out_specs=[pl.BlockSpec((narrow, total, depth), lambda at: (0, 0, 0)), whole, whole],
        out_shape=[
            jax.ShapeDtypeStruct((narrow, total, depth), jnp.float32),
            jax.ShapeDtypeStruct((rows, depth), jnp.bfloat16),
            jax.ShapeDtypeStruct((rows, depth), jnp.bfloat16),
        ],
        compiler_params=pltpu.CompilerParams(vmem_limit_bytes=VMEM_BYTES),
    )(normals, normals, counts, counts, normals, normals, counts, counts)


def halos_of(normals, counts):
    wide = lax.axis_size("wide")
    lines, first, last = edges_of(normals, counts, lax.axis_size("narrow"))
    lines = lax.all_to_all(lines, "narrow", split_axis=0, concat_axis=0, tiled=True)
    low_x = lax.ppermute(last, "wide", [(i, i + 1) for i in range(wide - 1)])
    high_x = lax.ppermute(first, "wide", [(i + 1, i) for i in range(wide - 1)])
    return lines, low_x, high_x


def per_device(normals, counts):
    wide = lax.axis_size("wide")
    narrow = lax.axis_size("narrow")
    _, total, rows, depth = normals.shape
    full_y = narrow * rows
    slab = depth // (wide * narrow)
    halos = halos_of(normals, counts)
    table_z = jnp.asarray(cosine_table(depth) * ml_dtypes.bfloat16(0.5))
    table_y = jnp.asarray(np.ascontiguousarray(cosine_table(full_y).T))
    cores = 2
    far = wide // cores
    near = cores * narrow
    if slab % 16 == 0 and total % 32 == 0 and wide == cores * far and far & (far - 1) == 0 and near & (near - 1) == 0:
        few = total // 4
        fewer = few // 2
        third = 3 * few
        first, second = third - fewer, 0
        pieces = along_z_of(normals, counts, halos, table_z, first, fewer, 1, wide * narrow)[0]
        pieces = after(pieces, *halos)
        first_pieces = pieces
        arrived = lax.all_to_all(pieces, ("wide", "narrow"), split_axis=0, concat_axis=0, tiled=True)
        later = after(table_z, pieces)
        pieces = along_z_of(normals, counts, halos, later, second, first, 1, wide * narrow)[0]
        pieces = after(pieces, arrived)
        arrived_later = lax.all_to_all(pieces, ("wide", "narrow"), split_axis=0, concat_axis=0, tiled=True)
        later = after(table_z, first_pieces)
        tiles = along_z_of(normals, counts, halos, later, third, few, near, 1, (far, near))
        tiles = [swap_near(tile[0], step, near) for step, tile in enumerate(tiles)]
        far_pieces = along_y_near(tiles, table_y, far, narrow)
        far_pieces = [swap_far(piece, step, near) for step, piece in enumerate(far_pieces)]
        spectrum = along_y_far([after(arrived_later, far_pieces[0]), arrived], table_y, total, narrow)
        for step, piece in enumerate(far_pieces):
            at = partner(device() // near, step) * cores
            spectrum = lax.dynamic_update_slice(spectrum, piece, (0, at, third, 0))
        return spectrum.reshape(slab, wide * total, full_y)
    along = along_z_of(normals, counts, halos, table_z, 0, total)[0]
    along = along.reshape(total, wide * narrow, slab, rows)
    arrived = lax.all_to_all(along, ("wide", "narrow"), split_axis=1, concat_axis=1, tiled=True)
    arrived = arrived.reshape(total, wide, narrow, slab, rows)
    pencil = jnp.transpose(arrived, (3, 1, 0, 2, 4)).reshape(slab * wide * total, full_y)
    spectrum = jnp.dot(pencil, table_y, preferred_element_type=jnp.float32).astype(jnp.bfloat16)
    return spectrum.reshape(slab, wide * total, full_y)


def solution(mesh):
    placed = (P(None, "wide", "narrow", None), P("wide", "narrow", None))
    return jax.shard_map(
        per_device,
        mesh=mesh,
        in_specs=placed,
        out_specs=P(("wide", "narrow"), None, None),
        check_vma=False,
    )
```
